32 devices in a mesh: seq: 8 (over z, x), head: 4 (over y, core).
Axes of the slice: x: 2, y: 2, z: 4, core: 2. Of those that a mesh axis runs over, the one named last changes fastest.
Arguments:
- tokens: bfloat16 [2048, 5376], P('seq'), may hold values from -6 to 6
- q_weight: bfloat16 [5376, 2048], P('seq', 'head')
- k_weight: bfloat16 [5376, 1024], P('seq', 'head')
- v_weight: bfloat16 [5376, 1024], P('seq', 'head'), may hold values from -0.078125 to 0.078125
- q_gain: float32 [128], replicated, may hold values from 0.5 to 6
- k_gain: float32 [128], replicated, may hold values from 0.5 to 6
- windows: int32 [16], P('head'), may hold values from 512 to 1024, as said below
- token_weight: float32 [2048], P('seq'), may hold values from 0.3 to 6
- loss_mask: int32 [2048], P('seq'), may hold values from 0 to 1, as said below
- grad_attn: bfloat16 [2048, 2048], P('seq', 'head'), may hold values from -6 to 6
Outputs:
- attn: bfloat16 [2048, 2048], P('seq', 'head')
- grad_tokens: bfloat16 [2048, 5376], P('seq', 'head')
The draws below stay inside these ranges and needn't reach their ends.
Inputs may be any that keep to these rules, and one draw needn't show every extreme that they name: `windows`: some head has a window of exactly 1024 keys and some head exactly 512. `loss_mask`: the first token always counts.
All inputs are finite; a program needn't handle non-finite values.
Results may differ from the reference program's by a relative error of at most 0.038.
The reference program's roundings to bfloat16 on the way count: a program that leaves them out, or rounds other values in their place, can miss the bound.
Values may be sent and summed in bfloat16 or wider, within the bound.
A program may use at most 128 MiB of HBM per device.

```python
import jax
import jax.numpy as jnp
from jax import lax

D = 5376
HQ = 16
KV = 8
HD = 128
QPRE = 168
WINDOW = 1024
TOK_DEV = 256
TOKENS = 2048


def query_matrix(key):
    base_key = jax.random.fold_in(key, 11)
    matrix = jax.random.normal(base_key, (D, HQ * HD), jnp.float32) * D ** (-0.5)
    return matrix


def draw_q_weight(key, part):
    return query_matrix(key).astype(jnp.bfloat16)


def draw_k_weight(key, part):
    noise = jax.random.normal(jax.random.fold_in(key, 12), (D, KV * HD), jnp.float32) * D ** (-0.5)
    result = noise
    return result.astype(jnp.bfloat16)


def gain_draw(key, salt):
    sub_key = jax.random.fold_in(key, salt)
    result = jax.random.uniform(sub_key, (HD,), jnp.float32, 0.5, 1.6)
    return result


def draw_q_gain(key, part):
    return gain_draw(key, 13)


def draw_k_gain(key, part):
    return gain_draw(key, 14)


def draw_token_weight(key, part):
    sub_key = jax.random.fold_in(key, 15)
    ramp = 1.0 + 2.0 * jnp.arange(TOKENS, dtype=jnp.float32) / TOKENS
    spread = jax.random.uniform(sub_key, (TOKENS,), jnp.float32, 0.5, 1.5)
    return spread * ramp


def draw_loss_mask(key, part):
    sub_key = jax.random.fold_in(key, 16)
    positions = jnp.arange(TOKENS, dtype=jnp.int32)
    thresholds = 300 + 600 * positions // TOKENS
    draws = jax.random.randint(sub_key, (TOKENS,), 0, 1000, dtype=jnp.int32)
    result = (draws < thresholds).astype(jnp.int32)
    return result.at[0].set(1)


def draw_windows(key, part):
    sub_key = jax.random.fold_in(key, 17)
    key_one, key_two, key_three = jax.random.split(sub_key, 3)
    lengths = jax.random.randint(key_one, (HQ,), WINDOW // 2, WINDOW + 1, dtype=jnp.int32)
    longest = jax.random.randint(key_two, (), 0, HQ, dtype=jnp.int32)
    shortest = (longest + 1 + jax.random.randint(key_three, (), 0, HQ - 1, dtype=jnp.int32)) % HQ
    return lengths.at[longest].set(WINDOW).at[shortest].set(WINDOW // 2)


def level_of(key, extent, cuts, smallest, top_value):
    def one(position, parts):
        heights = jax.random.uniform(jax.random.fold_in(jax.random.fold_in(key, 6), position), (parts,), jnp.float32, smallest / len(cuts), top_value / len(cuts))
        return jnp.repeat(jnp.exp(heights), extent[position] // parts).reshape((-1,) + (1,) * (len(extent) - position - 1))

    factor_of = one(*cuts[0])
    for cut in cuts[1:]:
        factor_of = factor_of * one(*cut)
    return factor_of


def normal_values(key, shape, scale, limit, cuts=(), held_as=jnp.bfloat16):
    values = scale * jax.random.normal(key, shape, jnp.float32)
    if cuts:
        values = values * level_of(key, shape, cuts, -0.22, 0.18)
    return jnp.clip(values, -limit, limit).astype(held_as)


def setup_inputs(seed: int = 0) -> dict:
    keys = jax.random.split(jax.random.key(seed), 11)
    return {
        "tokens": normal_values(keys[0], (TOKENS, D), 1.0, 6.0, ((0, 8),)),
        "q_weight": draw_q_weight(jax.random.fold_in(keys[10], 71), 0),
        "k_weight": draw_k_weight(jax.random.fold_in(keys[10], 71), 0),
        "v_weight": normal_values(keys[3], (D, KV * HD), D ** -0.5, 0.078125, ((0, 8), (1, 4))),
        "q_gain": draw_q_gain(jax.random.fold_in(keys[10], 71), 0),
        "k_gain": draw_k_gain(jax.random.fold_in(keys[10], 71), 0),
        "windows": draw_windows(jax.random.fold_in(keys[10], 71), 0),
        "token_weight": draw_token_weight(jax.random.fold_in(keys[10], 71), 0),
        "loss_mask": draw_loss_mask(jax.random.fold_in(keys[10], 71), 0),
        "grad_attn": normal_values(keys[9], (TOKENS, HQ * HD), 1.0, 6.0, ((0, 8), (1, 4))),
    }


norm_eps = 1e-06

def rotate_table(positions, head_width):
    half_width = head_width // 2
    frequency = 10000.0 ** (-(jnp.arange(half_width, dtype=jnp.float32) * 2.0) / head_width)
    angles = positions.astype(jnp.float32)[:, None] * frequency[None, :]
    return (jnp.cos(angles)[:, None, :], jnp.sin(angles)[:, None, :])

def norm_rotate(linear, gain_vec, cosine, sine_table):
    mean_square = lax.optimization_barrier(jnp.mean(linear * linear, axis=-1, keepdims=True))
    normed = linear * lax.rsqrt(mean_square + norm_eps) * gain_vec
    half_width = linear.shape[-1] // 2
    first_half = normed[..., :half_width]
    second_half = normed[..., half_width:]
    return jnp.concatenate([first_half * cosine - second_half * sine_table, second_half * cosine + first_half * sine_table], axis=-1)

def block_grad(queries, key_rows, value_rows, cotangent, query_pos, key_pos, windows, score_scale):
    tok_rows, q_heads, head_width = queries.shape
    kv_heads = key_rows.shape[1]
    group_size = q_heads // kv_heads
    query_grp = queries.reshape(tok_rows, kv_heads, group_size, head_width).astype(jnp.float32)
    cotan_grp = cotangent.reshape(tok_rows, kv_heads, group_size, head_width).astype(jnp.float32)
    key_float = key_rows.astype(jnp.float32)
    value_float = value_rows.astype(jnp.float32)
    scores = score_scale * jnp.einsum('tgjd,sgd->gjts', query_grp, key_float)
    distance = query_pos[:, None] - key_pos[None, :]
    reach = windows.reshape(kv_heads, group_size)[:, :, None, None]
    allowed = (distance[None, None] >= 0) & (distance[None, None] < reach) & (key_pos >= 0)[None, None, None, :]
    masked = jnp.where(allowed, scores, jnp.float32(-1e+30))
    row_peak = lax.optimization_barrier(jnp.max(masked, axis=-1, keepdims=True))
    row_total = lax.optimization_barrier(jnp.sum(jnp.where(allowed, jnp.exp(masked - row_peak), jnp.float32(0.0)), axis=-1, keepdims=True))
    logsum = row_peak + jnp.log(row_total)
    probability = jnp.where(allowed, jnp.exp(masked - logsum), jnp.float32(0.0))
    probs_b = probability.astype(jnp.bfloat16)
    attended = jnp.einsum('gjts,sgd->tgjd', probs_b.astype(jnp.float32), value_float).astype(jnp.bfloat16)
    row_delta = lax.optimization_barrier(jnp.sum(cotan_grp * attended.astype(jnp.float32), axis=-1))
    dprobs = jnp.einsum('tgjd,sgd->gjts', cotan_grp, value_float)
    dscore = (probability * (dprobs - jnp.transpose(row_delta, (1, 2, 0))[..., None])).astype(jnp.bfloat16)
    dscore_f = dscore.astype(jnp.float32)
    dquery = score_scale * jnp.einsum('gjts,sgd->tgjd', dscore_f, key_float)
    key_grads = score_scale * jnp.einsum('gjts,tgjd->sgd', dscore_f, query_grp)
    dvalues = jnp.einsum('gjts,tgjd->sgd', probs_b.astype(jnp.float32), cotan_grp)
    return (attended.reshape(tok_rows, q_heads * head_width), dquery.reshape(tok_rows, q_heads, head_width), key_grads, dvalues)

def reference(tokens, q_weight, k_weight, v_weight, q_gain, k_gain, windows, token_weight, loss_mask, grad_attn):
    score_scale = QPRE ** (-0.5)
    lead_rows = WINDOW // TOK_DEV * TOK_DEV
    key_span = lead_rows + TOK_DEV
    q_linear = jnp.dot(tokens, q_weight, preferred_element_type=jnp.float32).reshape(TOKENS, HQ, HD)
    k_linear = jnp.dot(tokens, k_weight, preferred_element_type=jnp.float32).reshape(TOKENS, KV, HD)
    values = jnp.dot(tokens, v_weight, preferred_element_type=jnp.float32).astype(jnp.bfloat16).reshape(TOKENS, KV, HD)
    positions = jnp.arange(TOKENS, dtype=jnp.int32)
    cosine, sine_table = rotate_table(positions, HD)
    q_rot = norm_rotate(q_linear, q_gain, cosine, sine_table).astype(jnp.bfloat16)
    k_rot = norm_rotate(k_linear, k_gain, cosine, sine_table).astype(jnp.bfloat16)
    kept_weight = token_weight * loss_mask.astype(jnp.float32)
    normalizer = jnp.sum(kept_weight)
    factor = kept_weight * (TOKENS / normalizer)
    cotangent = (grad_attn.astype(jnp.float32) * factor[:, None]).astype(jnp.bfloat16).reshape(TOKENS, HQ, HD)
    key_pad = jnp.concatenate([jnp.zeros((lead_rows, KV, HD), jnp.bfloat16), k_rot], axis=0)
    value_pad = jnp.concatenate([jnp.zeros((lead_rows, KV, HD), jnp.bfloat16), values], axis=0)

    def block_step(carried, block_idx):
        key_acc, value_acc = carried
        first_row = (block_idx * TOK_DEV).astype(jnp.int32)
        queries = lax.dynamic_slice_in_dim(q_rot, first_row, TOK_DEV, 0)
        cotan_rows = lax.dynamic_slice_in_dim(cotangent, first_row, TOK_DEV, 0)
        key_rows = lax.dynamic_slice_in_dim(key_pad, first_row, key_span, 0)
        value_rows = lax.dynamic_slice_in_dim(value_pad, first_row, key_span, 0)
        query_pos = first_row + jnp.arange(TOK_DEV, dtype=jnp.int32)
        key_pos = first_row - lead_rows + jnp.arange(key_span, dtype=jnp.int32)
        attended, dquery, key_grads, dvalues = block_grad(queries, key_rows, value_rows, cotan_rows, query_pos, key_pos, windows, score_scale)
        key_acc = lax.dynamic_update_slice_in_dim(key_acc, lax.dynamic_slice_in_dim(key_acc, first_row, key_span, 0) + key_grads, first_row, 0)
        value_acc = lax.dynamic_update_slice_in_dim(value_acc, lax.dynamic_slice_in_dim(value_acc, first_row, key_span, 0) + dvalues, first_row, 0)
        return ((key_acc, value_acc), (attended, dquery))
    zero_rows = jnp.zeros((lead_rows + TOKENS, KV, HD), jnp.float32)
    (key_acc, value_acc), (attended, dquery) = lax.scan(block_step, (zero_rows, zero_rows), jnp.arange(TOKENS // TOK_DEV, dtype=jnp.int32))
    attn = attended.reshape(TOKENS, HQ * HD)
    dquery = dquery.reshape(TOKENS, HQ, HD)
    _, back_query = jax.vjp(lambda linear_in: norm_rotate(linear_in, q_gain, cosine, sine_table), q_linear)
    _, back_key = jax.vjp(lambda linear_in: norm_rotate(linear_in, k_gain, cosine, sine_table), k_linear)
    dq_lin = back_query(dquery)[0].astype(jnp.bfloat16).reshape(TOKENS, HQ * HD)
    dk_lin = back_key(key_acc[lead_rows:])[0].astype(jnp.bfloat16).reshape(TOKENS, KV * HD)
    dv_lin = value_acc[lead_rows:].astype(jnp.bfloat16).reshape(TOKENS, KV * HD)
    contract = (((1,), (1,)), ((), ()))
    grad_sum = lax.dot_general(dq_lin, q_weight, contract, preferred_element_type=jnp.float32)
    grad_sum = grad_sum + lax.dot_general(dk_lin, k_weight, contract, preferred_element_type=jnp.float32)
    grad_sum = grad_sum + lax.dot_general(dv_lin, v_weight, contract, preferred_element_type=jnp.float32)
    return (attn, grad_sum.astype(jnp.bfloat16))
```

```python
import functools

import jax
import jax.numpy as jnp
from jax import lax
from jax.experimental import pallas as pl
from jax.experimental.pallas import tpu as pltpu
from jax.sharding import PartitionSpec as P

QPRE = 168
WINDOW = 1024
NORM_EPS = 1e-06
MESH = pl.DeviceIdType.MESH


def ring_place(index, n):
    return jnp.where(index % 2 == 0, index // 2, n - 1 - index // 2)


def ring_index(place, n):
    return jnp.where(place < n // 2, 2 * place, 2 * (n - 1 - place) + 1)


def row_cuts(rows, parts):
    if rows % 16 or rows < 16 * parts:
        return [(0, rows)]
    units = rows // 16
    edges = [16 * (units * i // parts) for i in range(parts + 1)]
    return [(a, b - a) for a, b in zip(edges, edges[1:])]


def ring_gather(n, jobs, me, send_sems, recv_sems, middle=None):
    place = ring_place(me, n)

    def at(distance):
        return ring_index(lax.rem(place + distance + n, n), n)

    def copy(step, job):
        source, dest, way = jobs[job]
        owner = at(-way * step)
        return pltpu.make_async_remote_copy(
            src_ref=dest(owner),
            dst_ref=dest(owner),
            send_sem=send_sems.at[step, job],
            recv_sem=recv_sems.at[step, job],
            device_id={"seq": at(way)},
            device_id_type=MESH,
        )

    def first(job):
        source, dest, way = jobs[job]
        return pltpu.make_async_remote_copy(
            src_ref=source,
            dst_ref=dest(me),
            send_sem=send_sems.at[0, job],
            recv_sem=recv_sems.at[0, job],
            device_id={"seq": at(way)},
            device_id_type=MESH,
        )

    for job in range(len(jobs)):
        first(job).start()
    if middle is not None:
        middle()

    def arrived(step, job):
        source, dest, way = jobs[job]
        owner = at(-way * (step + 1))
        return pltpu.make_async_remote_copy(
            src_ref=dest(owner),
            dst_ref=dest(owner),
            send_sem=send_sems.at[step, job],
            recv_sem=recv_sems.at[step, job],
            device_id={"seq": at(way)},
            device_id_type=MESH,
        )

    def body(step, carry):
        for job in range(len(jobs)):
            arrived(step - 1, job).wait_recv()
            copy(step, job).start()
        return carry

    lax.fori_loop(1, n - 1, body, 0)
    for job in range(len(jobs)):
        arrived(n - 2, job).wait_recv()

    def drain(step, carry):
        for job in range(len(jobs)):
            arrived(step, job).wait_send()
        return carry

    lax.fori_loop(0, n - 1, drain, 0)


def greet(peers):
    barrier = pltpu.get_barrier_semaphore()
    for peer in peers:
        pl.semaphore_signal(barrier, inc=1, device_id={"seq": peer}, device_id_type=MESH)
    pl.semaphore_wait(barrier, len(peers))


def greet_near(n, me, reach):
    barrier = pltpu.get_barrier_semaphore()
    for step in range(1, reach + 1):
        for peer, there in ((me + step, me + step < n), (me - step, me >= step)):

            @pl.when(there)
            def _():
                pl.semaphore_signal(barrier, inc=1, device_id={"seq": peer}, device_id_type=MESH)

    pl.semaphore_wait(barrier, jnp.minimum(me, reach) + jnp.minimum(n - 1 - me, reach))


def kv_gather_kernel(n, k_ref, v_ref, tile_ref, kv_out, tile_out, send, recv, local):
    me = lax.axis_index("seq")
    rows, width = k_ref.shape
    place = ring_place(me, n)
    greet([ring_index(lax.rem(place + d + n, n), n) for d in (1, -1)])
    own = [
        pltpu.make_async_copy(k_ref, kv_out.at[me, :, pl.ds(0, width)], local.at[0]),
        pltpu.make_async_copy(v_ref, kv_out.at[me, :, pl.ds(width, width)], local.at[1]),
        pltpu.make_async_copy(tile_ref, tile_out.at[me], local.at[2]),
    ]
    jobs = []
    for a, size in row_cuts(rows, 2):
        jobs.append(
            (
                k_ref.at[pl.ds(a, size)],
                lambda owner, a=a, size=size: kv_out.at[owner, pl.ds(a, size), pl.ds(0, width)],
                1,
            )
        )
        jobs.append(
            (
                v_ref.at[pl.ds(a, size)],
                lambda owner, a=a, size=size: kv_out.at[owner, pl.ds(a, size), pl.ds(width, width)],
                -1,
            )
        )
    jobs.append((tile_ref, lambda owner: tile_out.at[owner], 1))

    def middle():
        for c in own:
            c.start()

    ring_gather(n, jobs, me, send, recv, middle)
    for c in own:
        c.wait()


def kv_gather(n, k_weight, v_weight, tile):
    rows, width = k_weight.shape
    jobs = 2 * len(row_cuts(rows, 2)) + 1
    hbm = pl.BlockSpec(memory_space=pl.ANY)
    return pl.pallas_call(
        functools.partial(kv_gather_kernel, n),
        out_shape=[
            jax.ShapeDtypeStruct((n, rows, 2 * width), jnp.bfloat16),
            jax.ShapeDtypeStruct((n,) + tile.shape, jnp.float32),
        ],
        in_specs=[hbm] * 3,
        out_specs=[hbm] * 2,
        scratch_shapes=[
            pltpu.SemaphoreType.DMA((n - 1, jobs)),
            pltpu.SemaphoreType.DMA((n - 1, jobs)),
            pltpu.SemaphoreType.DMA((3,)),
        ],
        compiler_params=pltpu.CompilerParams(collective_id=0, has_side_effects=True),
    )(k_weight, v_weight, tile)


def near_copies(n, me, reach, way, source, dest, send, recv):
    result = []
    for step in range(reach, 0, -1):
        peer = me + way * step
        goes = peer < n if way > 0 else peer >= 0
        back = me - way * step
        comes = back >= 0 if way > 0 else back < n
        copy = pltpu.make_async_remote_copy(
            src_ref=source(step),
            dst_ref=dest(step),
            send_sem=send.at[step - 1],
            recv_sem=recv.at[step - 1],
            device_id={"seq": peer},
            device_id_type=MESH,
        )
        result.append((copy, goes, comes))
    return result


def start_near(copies):
    for copy, goes, _ in copies:
        pl.when(goes)(copy.start)


def finish_near(copies):
    for copy, goes, comes in copies:
        pl.when(goes)(copy.wait_send)
        pl.when(comes)(copy.wait_recv)


def q_gather_kernel(n, reach, q_ref, kv_ref, q_out, near_out, send, recv, nsend, nrecv, local):
    me = lax.axis_index("seq")
    rows = q_ref.shape[0]
    greet_near(n, me, reach)
    own = pltpu.make_async_copy(q_ref, q_out.at[me], local.at[0])
    copies = near_copies(
        n, me, reach, 1, lambda step: kv_ref, lambda step: near_out.at[step - 1], nsend, nrecv
    )
    cuts = row_cuts(rows, 4)
    jobs = []
    for i, (a, size) in enumerate(cuts):
        jobs.append(
            (
                q_ref.at[pl.ds(a, size)],
                lambda owner, a=a, size=size: q_out.at[owner, pl.ds(a, size)],
                1 if i % 2 == 0 else -1,
            )
        )

    start_near(copies)
    ring_gather(n, jobs, me, send, recv, own.start)
    own.wait()
    finish_near(copies)


def q_gather(n, reach, q_weight, kv_own):
    rows, width = q_weight.shape
    jobs = len(row_cuts(rows, 4))
    hbm = pl.BlockSpec(memory_space=pl.ANY)
    return pl.pallas_call(
        functools.partial(q_gather_kernel, n, reach),
        out_shape=[
            jax.ShapeDtypeStruct((n, rows, width), jnp.bfloat16),
            jax.ShapeDtypeStruct((reach,) + kv_own.shape, jnp.bfloat16),
        ],
        in_specs=[hbm] * 2,
        out_specs=[hbm] * 2,
        scratch_shapes=[
            pltpu.SemaphoreType.DMA((n - 1, jobs)),
            pltpu.SemaphoreType.DMA((n - 1, jobs)),
            pltpu.SemaphoreType.DMA((reach,)),
            pltpu.SemaphoreType.DMA((reach,)),
            pltpu.SemaphoreType.DMA((1,)),
        ],
        compiler_params=pltpu.CompilerParams(collective_id=1, has_side_effects=True),
    )(q_weight, kv_own)


def give_back_kernel(n, reach, near_ref, near_out, send, recv):
    me = lax.axis_index("seq")
    greet_near(n, me, reach)
    copies = near_copies(
        n,
        me,
        reach,
        -1,
        lambda step: near_ref.at[step - 1],
        lambda step: near_out.at[step - 1],
        send,
        recv,
    )
    start_near(copies)
    finish_near(copies)


def give_back(n, reach, near):
    hbm = pl.BlockSpec(memory_space=pl.ANY)
    return pl.pallas_call(
        functools.partial(give_back_kernel, n, reach),
        out_shape=jax.ShapeDtypeStruct(near.shape, jnp.bfloat16),
        in_specs=[hbm],
        out_specs=hbm,
        scratch_shapes=[
            pltpu.SemaphoreType.DMA((reach,)),
            pltpu.SemaphoreType.DMA((reach,)),
        ],
        compiler_params=pltpu.CompilerParams(collective_id=2, has_side_effects=True),
    )(near)


def swap_halves(x):
    half = x.shape[-1] // 2
    return jnp.concatenate([x[:, half:], x[:, :half]], axis=1)


def rotate(u, gain, cosine, sine):
    mean_square = jnp.mean(u * u, axis=-1, keepdims=True)
    m = u * lax.rsqrt(mean_square + NORM_EPS) * gain
    return m * cosine + swap_halves(m) * sine


def rotate_back(u, gain, cosine, sine, grad):
    r = lax.rsqrt(jnp.mean(u * u, axis=-1, keepdims=True) + NORM_EPS)
    dn = (grad * cosine + swap_halves(grad * sine)) * gain
    return r * dn - u * (r * r * r) * jnp.mean(u * dn, axis=-1, keepdims=True)


def kv_ready_kernel(lin_ref, gain_ref, cos_ref, sin_ref, out_ref):
    width = gain_ref.shape[1]
    half = lin_ref.shape[1] // 2
    for g in range(half // width):
        cols = slice(g * width, (g + 1) * width)
        out_ref[:, cols] = rotate(
            lin_ref[:, cols], gain_ref[...], cos_ref[...], sin_ref[...]
        ).astype(jnp.bfloat16)
    out_ref[:, half:] = lin_ref[:, half:].astype(jnp.bfloat16)


def kv_back_kernel(reach, own_ref, near_ref, there_ref, lin_ref, gain_ref, cos_ref, sin_ref, out_ref):
    width = gain_ref.shape[1]
    full = lin_ref.shape[1]
    half = full // 2
    for g in range(full // width):
        cols = slice(g * width, (g + 1) * width)
        total = own_ref[:, cols]
        for step in range(reach):
            part = near_ref[step, :, cols].astype(jnp.float32)
            total = total + jnp.where(there_ref[step] > 0, part, 0.0)
        if g * width < half:
            total = rotate_back(
                lin_ref[:, cols], gain_ref[...], cos_ref[...], sin_ref[...], total
            )
        out_ref[:, cols] = total.astype(jnp.bfloat16)


def attend_kernel(
    reach,
    kv_heads,
    scale,
    there_ref,
    windows_ref,
    lin_ref,
    own_ref,
    near_ref,
    grad_ref,
    factor_ref,
    gain_ref,
    cos_ref,
    sin_ref,
    attn_ref,
    dq_ref,
    down_ref,
    dnear_ref,
    keys,
    soft,
    acc,
):
    rows = own_ref.shape[0]
    width = gain_ref.shape[1]
    q_heads = lin_ref.shape[1] // width
    group = q_heads // kv_heads
    keys[0] = own_ref[...]
    for step in range(1, reach + 1):
        keys[step] = jnp.where(there_ref[step - 1] > 0, near_ref[step - 1], 0)
    acc[...] = jnp.zeros_like(acc)
    gap = lax.broadcasted_iota(jnp.int32, (rows, rows), 0) - lax.broadcasted_iota(
        jnp.int32, (rows, rows), 1
    )
    last = (((1,), (1,)), ((), ()))
    first = (((0,), (0,)), ((), ()))

    def head(h, carry):
        cols = pl.ds(pl.multiple_of(h * width, width), width)
        kcols = pl.ds(pl.multiple_of(h // group * width, width), width)
        vcols = pl.ds(pl.multiple_of((kv_heads + h // group) * width, width), width)
        u = lin_ref[:, cols]
        q = rotate(u, gain_ref[...], cos_ref[...], sin_ref[...]).astype(jnp.bfloat16)
        cot = (grad_ref[:, cols].astype(jnp.float32) * factor_ref[...]).astype(jnp.bfloat16)
        peak = jnp.full((rows, 1), -1e30, jnp.float32)
        for b in range(reach + 1):
            s = scale * lax.dot_general(
                q, keys[b, :, kcols], last, preferred_element_type=jnp.float32
            )
            distance = gap + b * rows
            limit = windows_ref[h]
            if b == 0:
                ok = (distance >= 0) & (distance < limit)
            else:
                ok = distance < jnp.where(there_ref[b - 1] > 0, limit, 0)
            s = jnp.where(ok, s, -1e30)
            soft[b] = s
            peak = jnp.maximum(peak, jnp.max(s, axis=-1, keepdims=True))
        total = jnp.zeros((rows, 1), jnp.float32)
        for b in range(reach + 1):
            e = jnp.exp(soft[b] - peak)
            soft[b] = e
            total = total + jnp.sum(e, axis=-1, keepdims=True)
        inverse = 1.0 / total
        out = jnp.zeros((rows, width), jnp.float32)
        for b in range(reach + 1):
            p = soft[b] * inverse
            soft[b] = p
            pb = p.astype(jnp.bfloat16)
            out = out + jnp.dot(pb, keys[b, :, vcols], preferred_element_type=jnp.float32)
            acc[b, :, vcols] += lax.dot_general(
                pb, cot, first, preferred_element_type=jnp.float32
            )
        out = out.astype(jnp.bfloat16)
        attn_ref[:, cols] = out
        delta = jnp.sum(
            cot.astype(jnp.float32) * out.astype(jnp.float32), axis=-1, keepdims=True
        )
        dq = jnp.zeros((rows, width), jnp.float32)
        for b in range(reach + 1):
            dp = lax.dot_general(
                cot, keys[b, :, vcols], last, preferred_element_type=jnp.float32
            )
            ds = (soft[b] * (dp - delta)).astype(jnp.bfloat16)
            dq = dq + jnp.dot(ds, keys[b, :, kcols], preferred_element_type=jnp.float32)
            acc[b, :, kcols] += scale * lax.dot_general(
                ds, q, first, preferred_element_type=jnp.float32
            )
        dq_ref[:, cols] = rotate_back(
            u, gain_ref[...], cos_ref[...], sin_ref[...], scale * dq
        ).astype(jnp.bfloat16)
        return carry

    lax.fori_loop(0, q_heads, head, 0)
    down_ref[...] = acc[0]
    for step in range(1, reach + 1):
        dnear_ref[step - 1] = acc[step].astype(jnp.bfloat16)


VMEM = pl.BlockSpec(memory_space=pltpu.VMEM)
SMEM = pl.BlockSpec(memory_space=pltpu.SMEM)
ROOM = pltpu.CompilerParams(vmem_limit_bytes=40 * 1024 * 1024)


def body(
    tokens,
    q_weight,
    k_weight,
    v_weight,
    q_gain,
    k_gain,
    windows,
    token_weight,
    loss_mask,
    grad_attn,
):
    n = lax.axis_size("seq")
    me = lax.axis_index("seq")
    tok_rows, depth = tokens.shape
    head_width = q_gain.shape[0]
    q_cols = q_weight.shape[1]
    kv_cols = 2 * k_weight.shape[1]
    kv_heads = k_weight.shape[1] // head_width
    reach = WINDOW // tok_rows
    scale = QPRE ** (-0.5)
    f32 = jnp.float32

    kept = token_weight * loss_mask.astype(f32)
    tile = jnp.broadcast_to(jnp.sum(kept), (8, 128))
    kv_full, tiles = kv_gather(n, k_weight, v_weight, tile)
    normalizer = jnp.sum(tiles[:, 0, 0])
    factor = (kept * (tok_rows * n / normalizer))[:, None]

    positions = me * tok_rows + jnp.arange(tok_rows, dtype=jnp.int32)
    half_width = head_width // 2
    frequency = 10000.0 ** (-(jnp.arange(half_width, dtype=f32) * 2.0) / head_width)
    angles = positions.astype(f32)[:, None] * frequency[None, :]
    cosine, sine = jnp.cos(angles), jnp.sin(angles)
    cosine = jnp.concatenate([cosine, cosine], axis=1)
    sine = jnp.concatenate([-sine, sine], axis=1)
    steps = jnp.arange(1, reach + 1, dtype=jnp.int32)
    before = (me >= steps).astype(jnp.int32)
    after = (me + steps < n).astype(jnp.int32)
    q_gain = q_gain[None, :]
    k_gain = k_gain[None, :]

    kv_matrix = kv_full.reshape(depth, kv_cols)
    kv_lin = jnp.dot(tokens, kv_matrix, preferred_element_type=f32)
    kv_own = pl.pallas_call(
        kv_ready_kernel,
        out_shape=jax.ShapeDtypeStruct((tok_rows, kv_cols), jnp.bfloat16),
        in_specs=[VMEM] * 4,
        out_specs=VMEM,
        compiler_params=ROOM,
    )(kv_lin, k_gain, cosine, sine)
    q_full, near = q_gather(n, reach, q_weight, kv_own)
    q_matrix = q_full.reshape(depth, q_cols)
    q_lin = jnp.dot(tokens, q_matrix, preferred_element_type=f32)
    attended, dq_lin, down, dnear = pl.pallas_call(
        functools.partial(attend_kernel, reach, kv_heads, scale),
        out_shape=[
            jax.ShapeDtypeStruct((tok_rows, q_cols), jnp.bfloat16),
            jax.ShapeDtypeStruct((tok_rows, q_cols), jnp.bfloat16),
            jax.ShapeDtypeStruct((tok_rows, kv_cols), f32),
            jax.ShapeDtypeStruct((reach, tok_rows, kv_cols), jnp.bfloat16),
        ],
        in_specs=[SMEM] * 2 + [VMEM] * 8,
        out_specs=[VMEM] * 4,
        scratch_shapes=[
            pltpu.VMEM((reach + 1, tok_rows, kv_cols), jnp.bfloat16),
            pltpu.VMEM((reach + 1, tok_rows, tok_rows), f32),
            pltpu.VMEM((reach + 1, tok_rows, kv_cols), f32),
        ],
        compiler_params=ROOM,
    )(before, windows, q_lin, kv_own, near, grad_attn, factor, q_gain, cosine, sine)
    returned = give_back(n, reach, dnear)
    dkv_lin = pl.pallas_call(
        functools.partial(kv_back_kernel, reach),
        out_shape=jax.ShapeDtypeStruct((tok_rows, kv_cols), jnp.bfloat16),
        in_specs=[VMEM, VMEM, SMEM] + [VMEM] * 4,
        out_specs=VMEM,
        compiler_params=ROOM,
    )(down, returned, after, kv_lin, k_gain, cosine, sine)
    contract = (((1,), (1,)), ((), ()))
    partial_grad = lax.dot_general(
        dq_lin, q_matrix, contract, preferred_element_type=f32
    ) + lax.dot_general(dkv_lin, kv_matrix, contract, preferred_element_type=f32)
    grad_tokens = lax.psum_scatter(
        partial_grad.astype(jnp.bfloat16), "head", scatter_dimension=1, tiled=True
    )
    return (attended, grad_tokens)


def solution(mesh):
    in_specs = (
        P("seq", None),
        P("seq", "head"),
        P("seq", "head"),
        P("seq", "head"),
        P(),
        P(),
        P("head"),
        P("seq"),
        P("seq"),
        P("seq", "head"),
    )
    out_specs = (P("seq", "head"), P("seq", "head"))
    return jax.shard_map(body, mesh=mesh, in_specs=in_specs, out_specs=out_specs, check_vma=False)
```

```python
import functools

import jax
import jax.numpy as jnp
from jax import lax
from jax.experimental import pallas as pl
from jax.experimental.pallas import tpu as pltpu
from jax.sharding import PartitionSpec as P

QPRE = 168
WINDOW = 1024
NORM_EPS = 1e-06
MESH = pl.DeviceIdType.MESH


def ring_place(index, n):
    return jnp.where(index % 2 == 0, index // 2, n - 1 - index // 2)


def ring_index(place, n):
    return jnp.where(place < n // 2, 2 * place, 2 * (n - 1 - place) + 1)


def row_cuts(rows, parts):
    if rows % 16 or rows < 16 * parts:
        return [(0, rows)]
    units = rows // 16
    edges = [16 * (units * i // parts) for i in range(parts + 1)]
    return [(a, b - a) for a, b in zip(edges, edges[1:])]


def ring_gather(n, jobs, me, send_sems, recv_sems, middle, later=None):
    place = ring_place(me, n)

    def at(distance):
        return ring_index(lax.rem(place + distance + n, n), n)

    def copy(step, job):
        source, dest, way = jobs[job]
        owner = at(-way * step)
        return pltpu.make_async_remote_copy(
            src_ref=dest(owner),
            dst_ref=dest(owner),
            send_sem=send_sems.at[step, job],
            recv_sem=recv_sems.at[step, job],
            device_id={"seq": at(way)},
            device_id_type=MESH,
        )

    def first(job):
        source, dest, way = jobs[job]
        return pltpu.make_async_remote_copy(
            src_ref=source,
            dst_ref=dest(me),
            send_sem=send_sems.at[0, job],
            recv_sem=recv_sems.at[0, job],
            device_id={"seq": at(way)},
            device_id_type=MESH,
        )

    for job in range(len(jobs)):
        first(job).start()
    middle()

    def arrived(step, job):
        source, dest, way = jobs[job]
        owner = at(-way * (step + 1))
        return pltpu.make_async_remote_copy(
            src_ref=dest(owner),
            dst_ref=dest(owner),
            send_sem=send_sems.at[step, job],
            recv_sem=recv_sems.at[step, job],
            device_id={"seq": at(way)},
            device_id_type=MESH,
        )

    def body(step, carry):
        for job in range(len(jobs)):
            arrived(step - 1, job).wait_recv()
            copy(step, job).start()
        return carry

    turn = n // 2 - 1
    lax.fori_loop(1, turn, body, 0)
    if later is not None:
        later()
    lax.fori_loop(turn, n - 1, body, 0)
    for job in range(len(jobs)):
        arrived(n - 2, job).wait_recv()

    def drain(step, carry):
        for job in range(len(jobs)):
            arrived(step, job).wait_send()
        return carry

    lax.fori_loop(0, n - 1, drain, 0)


def greet(peers):
    barrier = pltpu.get_barrier_semaphore()
    for peer in peers:
        pl.semaphore_signal(barrier, inc=1, device_id={"seq": peer}, device_id_type=MESH)
    pl.semaphore_wait(barrier, len(peers))


def greet_near(n, me):
    barrier = pltpu.get_barrier_semaphore()

    def signal(peer):
        pl.semaphore_signal(barrier, inc=1, device_id={"seq": peer}, device_id_type=MESH)

    signal(pair_of(me))

    @pl.when(me + 2 < n)
    def _():
        signal(me + 2)

    @pl.when(me >= 2)
    def _():
        signal(me - 2)

    pl.semaphore_wait(barrier, 1 + jnp.minimum(me // 2, 1) + jnp.minimum((n - 1 - me) // 2, 1))


def pair_of(me):
    return me + 1 - 2 * (me % 2)


def to_seq(source, dest, peer, send, recv):
    return pltpu.make_async_remote_copy(
        src_ref=source,
        dst_ref=dest,
        send_sem=send,
        recv_sem=recv,
        device_id={"seq": peer},
        device_id_type=MESH,
    )


def kv_gather_kernel(n, k_ref, v_ref, tile_ref, kv_out, tile_out, send, recv, local):
    me = lax.axis_index("seq")
    rows, width = k_ref.shape
    place = ring_place(me, n)
    greet([ring_index(lax.rem(place + d + n, n), n) for d in (1, -1)])
    own = [
        pltpu.make_async_copy(k_ref, kv_out.at[me, :, pl.ds(0, width)], local.at[0]),
        pltpu.make_async_copy(v_ref, kv_out.at[me, :, pl.ds(width, width)], local.at[1]),
        pltpu.make_async_copy(tile_ref, tile_out.at[me], local.at[2]),
    ]
    jobs = []
    for a, size in row_cuts(rows, 2):
        jobs.append(
            (
                k_ref.at[pl.ds(a, size)],
                lambda owner, a=a, size=size: kv_out.at[owner, pl.ds(a, size), pl.ds(0, width)],
                1,
            )
        )
        jobs.append(
            (
                v_ref.at[pl.ds(a, size)],
                lambda owner, a=a, size=size: kv_out.at[owner, pl.ds(a, size), pl.ds(width, width)],
                -1,
            )
        )
    jobs.append((tile_ref, lambda owner: tile_out.at[owner], 1))

    def middle():
        for c in own:
            c.start()

    ring_gather(n, jobs, me, send, recv, middle)
    for c in own:
        c.wait()


def kv_gather(n, k_weight, v_weight, tile):
    rows, width = k_weight.shape
    jobs = 2 * len(row_cuts(rows, 2)) + 1
    hbm = pl.BlockSpec(memory_space=pl.ANY)
    return pl.pallas_call(
        functools.partial(kv_gather_kernel, n),
        out_shape=[
            jax.ShapeDtypeStruct((n, rows, 2 * width), jnp.bfloat16),
            jax.ShapeDtypeStruct((n,) + tile.shape, jnp.float32),
        ],
        in_specs=[hbm] * 3,
        out_specs=[hbm] * 2,
        scratch_shapes=[
            pltpu.SemaphoreType.DMA((n - 1, jobs)),
            pltpu.SemaphoreType.DMA((n - 1, jobs)),
            pltpu.SemaphoreType.DMA((3,)),
        ],
        compiler_params=pltpu.CompilerParams(collective_id=0, has_side_effects=True),
    )(k_weight, v_weight, tile)


def q_gather_kernel(n, q_ref, kv_ref, q_out, near_out, send, recv, nsend, nrecv, local):
    me = lax.axis_index("seq")
    odd = me % 2
    rows = q_ref.shape[0]
    greet_near(n, me)
    own = pltpu.make_async_copy(q_ref, q_out.at[me], local.at[0])
    pair = pair_of(me)
    up = to_seq(kv_ref, near_out.at[1], me + 2, nsend.at[0], nrecv.at[1])
    across = to_seq(kv_ref, near_out.at[0], pair, nsend.at[1], nrecv.at[0])
    up_again = to_seq(near_out.at[1], near_out.at[3], me + 2, nsend.at[2], nrecv.at[3])
    slot = 2 - 2 * odd
    across_two = to_seq(near_out.at[1], near_out.at[slot], pair, nsend.at[3], nrecv.at[slot])
    across_four = to_seq(near_out.at[3], near_out.at[2], pair, nsend.at[4], nrecv.at[2])
    has_up = me + 2 < n
    jobs = []
    for i, (a, size) in enumerate(row_cuts(rows, 4)):
        jobs.append(
            (
                q_ref.at[pl.ds(a, size)],
                lambda owner, a=a, size=size: q_out.at[owner, pl.ds(a, size)],
                1 if i % 2 == 0 else -1,
            )
        )

    pl.when(has_up)(up.start)
    pl.when(odd == 0)(across.start)

    def middle():
        own.start()

        @pl.when(me >= 2)
        def _():
            up.wait_recv()
            across_two.start()
            pl.when(has_up)(up_again.start)

    def later():
        @pl.when(me >= 4)
        def _():
            up_again.wait_recv()
            pl.when(odd == 1)(across_four.start)

    ring_gather(n, jobs, me, send, recv, middle, later)
    own.wait()

    @pl.when(has_up)
    def _():
        up.wait_send()
        pl.when(me >= 2)(up_again.wait_send)

    pl.when(me >= 2)(across_two.wait_send)

    @pl.when(odd == 0)
    def _():
        across.wait_send()
        pl.when(me >= 2)(lambda: to_seq(kv_ref, near_out.at[0], pair, nsend.at[1], nrecv.at[0]).wait_recv())
        pl.when(me >= 4)(across_four.wait_recv)

    @pl.when(odd == 1)
    def _():
        across.wait_recv()
        pl.when(me >= 4)(across_four.wait_send)
        pl.when(me >= 2)(lambda: to_seq(kv_ref, near_out.at[2], pair, nsend.at[1], nrecv.at[2]).wait_recv())


def q_gather(n, reach, q_weight, kv_own):
    rows, width = q_weight.shape
    jobs = len(row_cuts(rows, 4))
    hbm = pl.BlockSpec(memory_space=pl.ANY)
    return pl.pallas_call(
        functools.partial(q_gather_kernel, n),
        out_shape=[
            jax.ShapeDtypeStruct((n, rows, width), jnp.bfloat16),
            jax.ShapeDtypeStruct((reach,) + kv_own.shape, jnp.bfloat16),
        ],
        in_specs=[hbm] * 2,
        out_specs=[hbm] * 2,
        scratch_shapes=[
            pltpu.SemaphoreType.DMA((n - 1, jobs)),
            pltpu.SemaphoreType.DMA((n - 1, jobs)),
            pltpu.SemaphoreType.DMA((5,)),
            pltpu.SemaphoreType.DMA((reach,)),
            pltpu.SemaphoreType.DMA((1,)),
        ],
        compiler_params=pltpu.CompilerParams(collective_id=1, has_side_effects=True),
    )(q_weight, kv_own)


CUTS = 4


def give_back_kernel(n, near_ref, down_ref, total_ref, beside, other, far_in, far, mid, mid_in, send, recv):
    me = lax.axis_index("seq")
    odd = me % 2
    pair = pair_of(me)
    size = near_ref.shape[1] // CUTS
    f32 = jnp.float32
    greet_near(n, me)

    def rows(i):
        return pl.ds(pl.multiple_of(i * size, size), size)

    def copies(i):
        r = rows(i)
        return (
            to_seq(near_ref.at[2 - 2 * odd, r], other.at[r], pair, send.at[0, i], recv.at[0, i]),
            to_seq(near_ref.at[2 * odd, r], beside.at[r], pair, send.at[1, i], recv.at[1, i]),
            to_seq(far.at[r], far_in.at[r], me - 2, send.at[2, i], recv.at[2, i]),
            to_seq(mid.at[r], mid_in.at[r], me - 2, send.at[3, i], recv.at[3, i]),
        )

    def loop(step):
        lax.fori_loop(0, CUTS, lambda i, c: (step(i), c)[1], 0)

    def begin(i):
        a, b, _, _ = copies(i)
        a.start()
        b.start()

    loop(begin)

    def send_far(i):
        a, _, c, _ = copies(i)
        r = rows(i)
        far[r] = near_ref[3, r]

        @pl.when(odd == 1)
        def _():
            a.wait_recv()
            far[r] = (near_ref[3, r].astype(f32) + other[r].astype(f32)).astype(jnp.bfloat16)

        pl.when(me >= 2)(c.start)

    loop(send_far)

    def send_mid(i):
        _, b, c, d = copies(i)
        r = rows(i)
        b.wait_recv()
        mid[r] = (near_ref[1, r].astype(f32) + beside[r].astype(f32)).astype(jnp.bfloat16)

        @pl.when(me + 2 < n)
        def _():
            c.wait_recv()
            mid[r] = (
                near_ref[1, r].astype(f32) + beside[r].astype(f32) + far_in[r].astype(f32)
            ).astype(jnp.bfloat16)

        pl.when(me >= 2)(d.start)

    loop(send_mid)

    def finish(i):
        a, b, c, d = copies(i)
        r = rows(i)
        total_ref[r] = down_ref[r]

        @pl.when(odd == 0)
        def _():
            a.wait_recv()
            total_ref[r] = down_ref[r] + other[r].astype(f32)

        @pl.when(me + 2 < n)
        def _():
            d.wait_recv()
            total_ref[r] = total_ref[r] + mid_in[r].astype(f32)

        a.wait_send()
        b.wait_send()

        @pl.when(me >= 2)
        def _():
            c.wait_send()
            d.wait_send()

    loop(finish)


def give_back(n, near, down):
    return pl.pallas_call(
        functools.partial(give_back_kernel, n),
        out_shape=jax.ShapeDtypeStruct(down.shape, jnp.float32),
        in_specs=[VMEM] * 2,
        out_specs=VMEM,
        scratch_shapes=[pltpu.VMEM(down.shape, jnp.bfloat16)] * 6
        + [pltpu.SemaphoreType.DMA((4, CUTS))] * 2,
        compiler_params=pltpu.CompilerParams(
            collective_id=2, has_side_effects=True, vmem_limit_bytes=40 * 1024 * 1024
        ),
    )(near, down)


def head_sum_kernel(part_ref, out_ref, from_core, stage, from_y, send, recv):
    h = lax.axis_index("head")
    core, y = h % 2, h // 2
    size = out_ref.shape[0] // CUTS
    f32 = jnp.float32
    mate = 2 * y + 1 - core
    across = 2 * (1 - y) + core
    barrier = pltpu.get_barrier_semaphore()
    for peer in (mate, across):
        pl.semaphore_signal(barrier, inc=1, device_id={"head": peer}, device_id_type=MESH)
    pl.semaphore_wait(barrier, 2)

    def rows(i):
        return pl.ds(pl.multiple_of(i * size, size), size)

    def to_head(source, dest, peer, kind, i):
        return pltpu.make_async_remote_copy(
            src_ref=source,
            dst_ref=dest,
            send_sem=send.at[kind, i],
            recv_sem=recv.at[kind, i],
            device_id={"head": peer},
            device_id_type=MESH,
        )

    def copies(i):
        r = rows(i)
        return (
            to_head(part_ref.at[2 * (1 - y) + 1 - core, r], from_core.at[0, r], mate, 0, i),
            to_head(part_ref.at[2 * y + 1 - core, r], from_core.at[1, r], mate, 1, i),
            to_head(stage.at[r], from_y.at[r], across, 2, i),
        )

    def loop(step):
        lax.fori_loop(0, CUTS, lambda i, c: (step(i), c)[1], 0)

    loop(lambda i: copies(i)[0].start())
    loop(lambda i: copies(i)[1].start())

    def pass_on(i):
        a, _, c = copies(i)
        r = rows(i)
        a.wait_recv()
        stage[r] = (
            part_ref[2 * (1 - y) + core, r].astype(f32) + from_core[0, r].astype(f32)
        ).astype(jnp.bfloat16)
        c.start()

    loop(pass_on)

    def finish(i):
        a, b, c = copies(i)
        r = rows(i)
        b.wait_recv()
        c.wait_recv()
        out_ref[r] = (
            part_ref[2 * y + core, r].astype(f32)
            + from_core[1, r].astype(f32)
            + from_y[r].astype(f32)
        ).astype(jnp.bfloat16)
        a.wait_send()
        b.wait_send()
        c.wait_send()

    loop(finish)


def head_sum(parts):
    block = parts.shape[1:]
    return pl.pallas_call(
        head_sum_kernel,
        out_shape=jax.ShapeDtypeStruct(block, jnp.bfloat16),
        in_specs=[VMEM],
        out_specs=VMEM,
        scratch_shapes=[
            pltpu.VMEM((2,) + block, jnp.bfloat16),
            pltpu.VMEM(block, jnp.bfloat16),
            pltpu.VMEM(block, jnp.bfloat16),
            pltpu.SemaphoreType.DMA((3, CUTS)),
            pltpu.SemaphoreType.DMA((3, CUTS)),
        ],
        compiler_params=pltpu.CompilerParams(
            collective_id=3, has_side_effects=True, vmem_limit_bytes=40 * 1024 * 1024
        ),
    )(parts)


def swap_halves(x):
    half = x.shape[-1] // 2
    return jnp.concatenate([x[:, half:], x[:, :half]], axis=1)


def rotate(u, gain, cosine, sine):
    mean_square = jnp.mean(u * u, axis=-1, keepdims=True)
    m = u * lax.rsqrt(mean_square + NORM_EPS) * gain
    return m * cosine + swap_halves(m) * sine


def rotate_back(u, gain, cosine, sine, grad):
    r = lax.rsqrt(jnp.mean(u * u, axis=-1, keepdims=True) + NORM_EPS)
    dn = (grad * cosine + swap_halves(grad * sine)) * gain
    return r * dn - u * (r * r * r) * jnp.mean(u * dn, axis=-1, keepdims=True)


def kv_ready_kernel(
    tokens_total, lin_ref, gain_ref, cos_ref, sin_ref, tiles_ref, kept_ref, grad_ref, out_ref, cot_ref
):
    width = gain_ref.shape[1]
    half = lin_ref.shape[1] // 2
    for g in range(half // width):
        cols = slice(g * width, (g + 1) * width)
        out_ref[:, cols] = rotate(
            lin_ref[:, cols], gain_ref[...], cos_ref[...], sin_ref[...]
        ).astype(jnp.bfloat16)
    out_ref[:, half:] = lin_ref[:, half:].astype(jnp.bfloat16)
    normalizer = jnp.sum(tiles_ref[...], axis=0)[0:1, 0:1]
    factor = kept_ref[...] * (tokens_total / normalizer)
    cot_ref[...] = (grad_ref[...].astype(jnp.float32) * factor).astype(jnp.bfloat16)


def back_kernel(
    total_ref, lin_ref, gain_ref, cos_ref, sin_ref, dq_ref, q_mat, kv_mat, out_ref, dkv
):
    width = gain_ref.shape[1]
    full = lin_ref.shape[1]
    half = full // 2
    for g in range(half // width):
        cols = slice(g * width, (g + 1) * width)
        dkv[:, cols] = rotate_back(
            lin_ref[:, cols], gain_ref[...], cos_ref[...], sin_ref[...], total_ref[:, cols]
        ).astype(jnp.bfloat16)
    dkv[:, half:] = total_ref[:, half:].astype(jnp.bfloat16)
    last = (((1,), (1,)), ((), ()))

    def quarter(i, carry):
        out_ref[i] = (
            lax.dot_general(dq_ref[...], q_mat[i], last, preferred_element_type=jnp.float32)
            + lax.dot_general(dkv[...], kv_mat[i], last, preferred_element_type=jnp.float32)
        ).astype(jnp.bfloat16)
        return carry

    lax.fori_loop(0, out_ref.shape[0], quarter, 0)


def attend_kernel(
    reach,
    kv_heads,
    scale,
    there_ref,
    windows_ref,
    lin_ref,
    own_ref,
    near_ref,
    cot_ref,
    gain_ref,
    cos_ref,
    sin_ref,
    attn_ref,
    dq_ref,
    down_ref,
    dnear_ref,
    keys,
    soft,
    acc,
):
    rows = own_ref.shape[0]
    width = gain_ref.shape[1]
    q_heads = lin_ref.shape[1] // width
    group = q_heads // kv_heads
    keys[0] = own_ref[...]
    for step in range(1, reach + 1):
        keys[step] = jnp.where(there_ref[step - 1] > 0, near_ref[step - 1], 0)
    acc[...] = jnp.zeros_like(acc)
    gap = lax.broadcasted_iota(jnp.int32, (rows, rows), 0) - lax.broadcasted_iota(
        jnp.int32, (rows, rows), 1
    )
    last = (((1,), (1,)), ((), ()))
    first = (((0,), (0,)), ((), ()))

    def head(h, carry):
        cols = pl.ds(pl.multiple_of(h * width, width), width)
        kcols = pl.ds(pl.multiple_of(h // group * width, width), width)
        vcols = pl.ds(pl.multiple_of((kv_heads + h // group) * width, width), width)
        u = lin_ref[:, cols]
        q = rotate(u, gain_ref[...], cos_ref[...], sin_ref[...]).astype(jnp.bfloat16)
        cot = cot_ref[:, cols]
        peak = jnp.full((rows, 1), -1e30, jnp.float32)
        for b in range(reach + 1):
            s = scale * lax.dot_general(
                q, keys[b, :, kcols], last, preferred_element_type=jnp.float32
            )
            distance = gap + b * rows
            limit = windows_ref[h]
            if b == 0:
                ok = (distance >= 0) & (distance < limit)
            else:
                ok = distance < jnp.where(there_ref[b - 1] > 0, limit, 0)
            s = jnp.where(ok, s, -1e30)
            soft[b] = s
            peak = jnp.maximum(peak, jnp.max(s, axis=-1, keepdims=True))
        total = jnp.zeros((rows, 1), jnp.float32)
        for b in range(reach + 1):
            e = jnp.exp(soft[b] - peak)
            soft[b] = e
            total = total + jnp.sum(e, axis=-1, keepdims=True)
        inverse = 1.0 / total
        out = jnp.zeros((rows, width), jnp.float32)
        for b in range(reach + 1):
            p = soft[b] * inverse
            soft[b] = p
            pb = p.astype(jnp.bfloat16)
            out = out + jnp.dot(pb, keys[b, :, vcols], preferred_element_type=jnp.float32)
            acc[b, :, vcols] += lax.dot_general(
                pb, cot, first, preferred_element_type=jnp.float32
            )
        out = out.astype(jnp.bfloat16)
        attn_ref[:, cols] = out
        delta = jnp.sum(
            cot.astype(jnp.float32) * out.astype(jnp.float32), axis=-1, keepdims=True
        )
        dq = jnp.zeros((rows, width), jnp.float32)
        for b in range(reach + 1):
            dp = lax.dot_general(
                cot, keys[b, :, vcols], last, preferred_element_type=jnp.float32
            )
            ds = (soft[b] * (dp - delta)).astype(jnp.bfloat16)
            dq = dq + jnp.dot(ds, keys[b, :, kcols], preferred_element_type=jnp.float32)
            acc[b, :, kcols] += scale * lax.dot_general(
                ds, q, first, preferred_element_type=jnp.float32
            )
        dq_ref[:, cols] = rotate_back(
            u, gain_ref[...], cos_ref[...], sin_ref[...], scale * dq
        ).astype(jnp.bfloat16)
        return carry

    lax.fori_loop(0, q_heads, head, 0)
    down_ref[...] = acc[0]
    for step in range(1, reach + 1):
        dnear_ref[step - 1] = acc[step].astype(jnp.bfloat16)


VMEM = pl.BlockSpec(memory_space=pltpu.VMEM)
SMEM = pl.BlockSpec(memory_space=pltpu.SMEM)
ROOM = pltpu.CompilerParams(vmem_limit_bytes=40 * 1024 * 1024)


def body(
    tokens,
    q_weight,
    k_weight,
    v_weight,
    q_gain,
    k_gain,
    windows,
    token_weight,
    loss_mask,
    grad_attn,
):
    n = lax.axis_size("seq")
    me = lax.axis_index("seq")
    tok_rows, depth = tokens.shape
    head_width = q_gain.shape[0]
    q_cols = q_weight.shape[1]
    kv_cols = 2 * k_weight.shape[1]
    kv_heads = k_weight.shape[1] // head_width
    reach = WINDOW // tok_rows
    scale = QPRE ** (-0.5)
    f32 = jnp.float32

    kept = token_weight * loss_mask.astype(f32)
    tile = jnp.broadcast_to(jnp.sum(kept), (8, 128))
    kv_full, tiles = kv_gather(n, k_weight, v_weight, tile)
    positions = me * tok_rows + jnp.arange(tok_rows, dtype=jnp.int32)
    half_width = head_width // 2
    frequency = 10000.0 ** (-(jnp.arange(half_width, dtype=f32) * 2.0) / head_width)
    angles = positions.astype(f32)[:, None] * frequency[None, :]
    cosine, sine = jnp.cos(angles), jnp.sin(angles)
    cosine = jnp.concatenate([cosine, cosine], axis=1)
    sine = jnp.concatenate([-sine, sine], axis=1)
    steps = jnp.arange(1, reach + 1, dtype=jnp.int32)
    before = (me >= steps).astype(jnp.int32)
    q_gain = q_gain[None, :]
    k_gain = k_gain[None, :]

    kv_matrix = kv_full.reshape(depth, kv_cols)
    kv_lin = jnp.dot(tokens, kv_matrix, preferred_element_type=f32)
    kv_own, cot = pl.pallas_call(
        functools.partial(kv_ready_kernel, float(tok_rows * n)),
        out_shape=[
            jax.ShapeDtypeStruct((tok_rows, kv_cols), jnp.bfloat16),
            jax.ShapeDtypeStruct((tok_rows, q_cols), jnp.bfloat16),
        ],
        in_specs=[VMEM] * 7,
        out_specs=[VMEM] * 2,
        compiler_params=ROOM,
    )(kv_lin, k_gain, cosine, sine, tiles, kept[:, None], grad_attn)
    q_full, near = q_gather(n, reach, q_weight, kv_own)
    q_matrix = q_full.reshape(depth, q_cols)
    q_lin = jnp.dot(tokens, q_matrix, preferred_element_type=f32)
    attended, dq_lin, down, dnear = pl.pallas_call(
        functools.partial(attend_kernel, reach, kv_heads, scale),
        out_shape=[
            jax.ShapeDtypeStruct((tok_rows, q_cols), jnp.bfloat16),
            jax.ShapeDtypeStruct((tok_rows, q_cols), jnp.bfloat16),
            jax.ShapeDtypeStruct((tok_rows, kv_cols), f32),
            jax.ShapeDtypeStruct((reach, tok_rows, kv_cols), jnp.bfloat16),
        ],
        in_specs=[SMEM] * 2 + [VMEM] * 7,
        out_specs=[VMEM] * 4,
        scratch_shapes=[
            pltpu.VMEM((reach + 1, tok_rows, kv_cols), jnp.bfloat16),
            pltpu.VMEM((reach + 1, tok_rows, tok_rows), f32),
            pltpu.VMEM((reach + 1, tok_rows, kv_cols), f32),
        ],
        compiler_params=ROOM,
    )(before, windows, q_lin, kv_own, near, cot, q_gain, cosine, sine)
    total = give_back(n, dnear, down)
    heads = lax.axis_size("head")
    parts = pl.pallas_call(
        back_kernel,
        out_shape=jax.ShapeDtypeStruct((heads, tok_rows, depth // heads), jnp.bfloat16),
        in_specs=[VMEM] * 8,
        out_specs=VMEM,
        scratch_shapes=[pltpu.VMEM((tok_rows, kv_cols), jnp.bfloat16)],
        compiler_params=ROOM,
    )(
        total,
        kv_lin,
        k_gain,
        cosine,
        sine,
        dq_lin,
        q_full.reshape(heads, depth // heads, q_cols),
        kv_full.reshape(heads, depth // heads, kv_cols),
    )
    grad_tokens = head_sum(parts)
    return (attended, grad_tokens)


def solution(mesh):
    in_specs = (
        P("seq", None),
        P("seq", "head"),
        P("seq", "head"),
        P("seq", "head"),
        P(),
        P(),
        P("head"),
        P("seq"),
        P("seq"),
        P("seq", "head"),
    )
    out_specs = (P("seq", "head"), P("seq", "head"))
    return jax.shard_map(body, mesh=mesh, in_specs=in_specs, out_specs=out_specs, check_vma=False)
```

```python
import functools

import jax
import jax.numpy as jnp
from jax import lax
from jax.experimental import pallas as pl
from jax.experimental.pallas import tpu as pltpu
from jax.sharding import PartitionSpec as P

QPRE = 168
WINDOW = 1024
NORM_EPS = 1e-06
MESH = pl.DeviceIdType.MESH


def ring_place(index, n):
    return jnp.where(index % 2 == 0, index // 2, n - 1 - index // 2)


def ring_index(place, n):
    return jnp.where(place < n // 2, 2 * place, 2 * (n - 1 - place) + 1)


def row_cuts(rows, parts):
    if rows % 16 or rows < 16 * parts:
        return [(0, rows)]
    units = rows // 16
    edges = [16 * (units * i // parts) for i in range(parts + 1)]
    return [(a, b - a) for a, b in zip(edges, edges[1:])]


def ring_gather(n, jobs, me, send_sems, recv_sems, middle, later=None):
    place = ring_place(me, n)

    def at(distance):
        return ring_index(lax.rem(place + distance + n, n), n)

    def copy(step, job):
        source, dest, way = jobs[job]
        owner = at(-way * step)
        return pltpu.make_async_remote_copy(
            src_ref=dest(owner),
            dst_ref=dest(owner),
            send_sem=send_sems.at[step, job],
            recv_sem=recv_sems.at[step, job],
            device_id={"seq": at(way)},
            device_id_type=MESH,
        )

    def first(job):
        source, dest, way = jobs[job]
        return pltpu.make_async_remote_copy(
            src_ref=source,
            dst_ref=dest(me),
            send_sem=send_sems.at[0, job],
            recv_sem=recv_sems.at[0, job],
            device_id={"seq": at(way)},
            device_id_type=MESH,
        )

    for job in range(len(jobs)):
        first(job).start()
    middle()

    def arrived(step, job):
        source, dest, way = jobs[job]
        owner = at(-way * (step + 1))
        return pltpu.make_async_remote_copy(
            src_ref=dest(owner),
            dst_ref=dest(owner),
            send_sem=send_sems.at[step, job],
            recv_sem=recv_sems.at[step, job],
            device_id={"seq": at(way)},
            device_id_type=MESH,
        )

    def body(step, carry):
        for job in range(len(jobs)):
            arrived(step - 1, job).wait_recv()
            copy(step, job).start()
        return carry

    turn = n // 2 - 1
    lax.fori_loop(1, turn, body, 0)
    if later is not None:
        later()
    lax.fori_loop(turn, n - 1, body, 0)
    for job in range(len(jobs)):
        arrived(n - 2, job).wait_recv()

    def drain(step, carry):
        for job in range(len(jobs)):
            arrived(step, job).wait_send()
        return carry

    lax.fori_loop(0, n - 1, drain, 0)


def greet(peers):
    barrier = pltpu.get_barrier_semaphore()
    for peer in peers:
        pl.semaphore_signal(barrier, inc=1, device_id={"seq": peer}, device_id_type=MESH)
    pl.semaphore_wait(barrier, len(peers))


def greet_near(n, me, more=0):
    barrier = pltpu.get_barrier_semaphore()

    def signal(peer):
        pl.semaphore_signal(barrier, inc=1, device_id={"seq": peer}, device_id_type=MESH)

    signal(pair_of(me))

    @pl.when(me + 2 < n)
    def _():
        signal(me + 2)

    @pl.when(me >= 2)
    def _():
        signal(me - 2)

    pl.semaphore_wait(barrier, more + 1 + jnp.minimum(me // 2, 1) + jnp.minimum((n - 1 - me) // 2, 1))


def pair_of(me):
    return me + 1 - 2 * (me % 2)


def to_seq(source, dest, peer, send, recv):
    return pltpu.make_async_remote_copy(
        src_ref=source,
        dst_ref=dest,
        send_sem=send,
        recv_sem=recv,
        device_id={"seq": peer},
        device_id_type=MESH,
    )


def kv_gather_kernel(n, k_ref, v_ref, tile_ref, kv_out, tile_out, send, recv, local):
    me = lax.axis_index("seq")
    rows, width = k_ref.shape
    place = ring_place(me, n)
    greet([ring_index(lax.rem(place + d + n, n), n) for d in (1, -1)])
    own = [
        pltpu.make_async_copy(k_ref, kv_out.at[me, :, pl.ds(0, width)], local.at[0]),
        pltpu.make_async_copy(v_ref, kv_out.at[me, :, pl.ds(width, width)], local.at[1]),
        pltpu.make_async_copy(tile_ref, tile_out.at[me], local.at[2]),
    ]
    jobs = []
    for a, size in row_cuts(rows, 2):
        jobs.append(
            (
                k_ref.at[pl.ds(a, size)],
                lambda owner, a=a, size=size: kv_out.at[owner, pl.ds(a, size), pl.ds(0, width)],
                1,
            )
        )
        jobs.append(
            (
                v_ref.at[pl.ds(a, size)],
                lambda owner, a=a, size=size: kv_out.at[owner, pl.ds(a, size), pl.ds(width, width)],
                -1,
            )
        )
    jobs.append((tile_ref, lambda owner: tile_out.at[owner], 1))

    def middle():
        for c in own:
            c.start()

    ring_gather(n, jobs, me, send, recv, middle)
    for c in own:
        c.wait()


def kv_gather(n, k_weight, v_weight, tile):
    rows, width = k_weight.shape
    jobs = 2 * len(row_cuts(rows, 2)) + 1
    hbm = pl.BlockSpec(memory_space=pl.ANY)
    return pl.pallas_call(
        functools.partial(kv_gather_kernel, n),
        out_shape=[
            jax.ShapeDtypeStruct((n, rows, 2 * width), jnp.bfloat16),
            jax.ShapeDtypeStruct((n,) + tile.shape, jnp.float32),
        ],
        in_specs=[hbm] * 3,
        out_specs=[hbm] * 2,
        scratch_shapes=[
            pltpu.SemaphoreType.DMA((n - 1, jobs)),
            pltpu.SemaphoreType.DMA((n - 1, jobs)),
            pltpu.SemaphoreType.DMA((3,)),
        ],
        compiler_params=pltpu.CompilerParams(collective_id=0, has_side_effects=True),
    )(k_weight, v_weight, tile)


def q_gather_kernel(n, q_ref, kv_ref, q_out, near_out, send, recv, nsend, nrecv, local):
    me = lax.axis_index("seq")
    odd = me % 2
    rows = q_ref.shape[0]
    greet_near(n, me)
    own = pltpu.make_async_copy(q_ref, q_out.at[me], local.at[0])
    pair = pair_of(me)
    up = to_seq(kv_ref, near_out.at[1], me + 2, nsend.at[0], nrecv.at[1])
    across = to_seq(kv_ref, near_out.at[0], pair, nsend.at[1], nrecv.at[0])
    up_again = to_seq(near_out.at[1], near_out.at[3], me + 2, nsend.at[2], nrecv.at[3])
    slot = 2 - 2 * odd
    across_two = to_seq(near_out.at[1], near_out.at[slot], pair, nsend.at[3], nrecv.at[slot])
    across_four = to_seq(near_out.at[3], near_out.at[2], pair, nsend.at[4], nrecv.at[2])
    has_up = me + 2 < n
    jobs = []
    for i, (a, size) in enumerate(row_cuts(rows, 4)):
        jobs.append(
            (
                q_ref.at[pl.ds(a, size)],
                lambda owner, a=a, size=size: q_out.at[owner, pl.ds(a, size)],
                1 if i % 2 == 0 else -1,
            )
        )

    pl.when(has_up)(up.start)
    pl.when(odd == 0)(across.start)

    def middle():
        own.start()

        @pl.when(me >= 2)
        def _():
            up.wait_recv()
            across_two.start()
            pl.when(has_up)(up_again.start)

    def later():
        @pl.when(me >= 4)
        def _():
            up_again.wait_recv()
            pl.when(odd == 1)(across_four.start)

    ring_gather(n, jobs, me, send, recv, middle, later)
    own.wait()

    @pl.when(has_up)
    def _():
        up.wait_send()
        pl.when(me >= 2)(up_again.wait_send)

    pl.when(me >= 2)(across_two.wait_send)

    @pl.when(odd == 0)
    def _():
        across.wait_send()
        pl.when(me >= 2)(lambda: to_seq(kv_ref, near_out.at[0], pair, nsend.at[1], nrecv.at[0]).wait_recv())
        pl.when(me >= 4)(across_four.wait_recv)

    @pl.when(odd == 1)
    def _():
        across.wait_recv()
        pl.when(me >= 4)(across_four.wait_send)
        pl.when(me >= 2)(lambda: to_seq(kv_ref, near_out.at[2], pair, nsend.at[1], nrecv.at[2]).wait_recv())


def q_gather(n, reach, q_weight, kv_own):
    rows, width = q_weight.shape
    jobs = len(row_cuts(rows, 4))
    hbm = pl.BlockSpec(memory_space=pl.ANY)
    return pl.pallas_call(
        functools.partial(q_gather_kernel, n),
        out_shape=[
            jax.ShapeDtypeStruct((n, rows, width), jnp.bfloat16),
            jax.ShapeDtypeStruct((reach,) + kv_own.shape, jnp.bfloat16),
        ],
        in_specs=[hbm] * 2,
        out_specs=[hbm] * 2,
        scratch_shapes=[
            pltpu.SemaphoreType.DMA((n - 1, jobs)),
            pltpu.SemaphoreType.DMA((n - 1, jobs)),
            pltpu.SemaphoreType.DMA((5,)),
            pltpu.SemaphoreType.DMA((reach,)),
            pltpu.SemaphoreType.DMA((1,)),
        ],
        compiler_params=pltpu.CompilerParams(collective_id=1, has_side_effects=True),
    )(q_weight, kv_own)


CUTS = 4


def swap_halves(x):
    half = x.shape[-1] // 2
    return jnp.concatenate([x[:, half:], x[:, :half]], axis=1)


def rotate(u, gain, cosine, sine):
    mean_square = jnp.mean(u * u, axis=-1, keepdims=True)
    m = u * lax.rsqrt(mean_square + NORM_EPS) * gain
    return m * cosine + swap_halves(m) * sine


def rotate_back(u, gain, cosine, sine, grad):
    r = lax.rsqrt(jnp.mean(u * u, axis=-1, keepdims=True) + NORM_EPS)
    dn = (grad * cosine + swap_halves(grad * sine)) * gain
    return r * dn - u * (r * r * r) * jnp.mean(u * dn, axis=-1, keepdims=True)


def kv_ready_kernel(
    tokens_total, lin_ref, gain_ref, cos_ref, sin_ref, tiles_ref, kept_ref, grad_ref, out_ref, cot_ref
):
    width = gain_ref.shape[1]
    half = lin_ref.shape[1] // 2
    for g in range(half // width):
        cols = slice(g * width, (g + 1) * width)
        out_ref[:, cols] = rotate(
            lin_ref[:, cols], gain_ref[...], cos_ref[...], sin_ref[...]
        ).astype(jnp.bfloat16)
    out_ref[:, half:] = lin_ref[:, half:].astype(jnp.bfloat16)
    normalizer = jnp.sum(tiles_ref[...], axis=0)[0:1, 0:1]
    factor = kept_ref[...] * (tokens_total / normalizer)
    cot_ref[...] = (grad_ref[...].astype(jnp.float32) * factor).astype(jnp.bfloat16)


def tail_kernel(
    n,
    near_ref,
    down_ref,
    lin_ref,
    gain_ref,
    cos_ref,
    sin_ref,
    dq_ref,
    q_hbm,
    kv_hbm,
    out_ref,
    q_mat,
    kv_mat,
    total,
    part,
    own,
    beside,
    other,
    far_in,
    far,
    mid,
    mid_in,
    from_core,
    stage,
    from_y,
    send,
    recv,
    hsend,
    hrecv,
    local,
):
    me = lax.axis_index("seq")
    odd = me % 2
    pair = pair_of(me)
    h = lax.axis_index("head")
    core, y = h % 2, h // 2
    mate = 2 * y + 1 - core
    across = 2 * (1 - y) + core
    size = near_ref.shape[1] // CUTS
    width = gain_ref.shape[1]
    half = lin_ref.shape[1] // 2
    f32 = jnp.float32
    last = (((1,), (1,)), ((), ()))
    q_copy = pltpu.make_async_copy(q_hbm, q_mat, local.at[0])
    kv_copy = pltpu.make_async_copy(kv_hbm, kv_mat, local.at[1])
    q_copy.start()
    kv_copy.start()
    barrier = pltpu.get_barrier_semaphore()
    for peer in (mate, across):
        pl.semaphore_signal(barrier, inc=1, device_id={"head": peer}, device_id_type=MESH)
    greet_near(n, me, 2)

    def rows(i):
        return pl.ds(pl.multiple_of(i * size, size), size)

    def to_head(source, dest, peer, kind, i):
        return pltpu.make_async_remote_copy(
            src_ref=source,
            dst_ref=dest,
            send_sem=hsend.at[kind, i],
            recv_sem=hrecv.at[kind, i],
            device_id={"head": peer},
            device_id_type=MESH,
        )

    def other_copy(i):
        r = rows(i)
        return to_seq(near_ref.at[2 - 2 * odd, r], other.at[r], pair, send.at[0, i], recv.at[0, i])

    def beside_copy(i):
        r = rows(i)
        return to_seq(near_ref.at[2 * odd, r], beside.at[r], pair, send.at[1, i], recv.at[1, i])

    def far_copy(i):
        r = rows(i)
        return to_seq(far.at[r], far_in.at[r], me - 2, send.at[2, i], recv.at[2, i])

    def mid_copy(i):
        r = rows(i)
        return to_seq(mid.at[r], mid_in.at[r], me - 2, send.at[3, i], recv.at[3, i])

    pass_q, keep_q = 2 * (1 - y) + core, 2 * y + core
    mate_pass_q, mate_keep_q = 2 * (1 - y) + 1 - core, 2 * y + 1 - core

    def mate_pass_copy(i):
        r = rows(i)
        return to_head(part.at[mate_pass_q, r], from_core.at[0, r], mate, 0, i)

    def mate_keep_copy(i):
        r = rows(i)
        return to_head(part.at[mate_keep_q, r], from_core.at[1, r], mate, 1, i)

    def y_copy(i):
        r = rows(i)
        return to_head(stage.at[r], from_y.at[r], across, 2, i)

    def loop(step):
        lax.fori_loop(0, CUTS, lambda i, c: (step(i), c)[1], 0)

    def begin(i):
        other_copy(i).start()
        beside_copy(i).start()

    loop(begin)

    def send_far(i):
        r = rows(i)
        far[r] = near_ref[3, r]

        @pl.when(odd == 1)
        def _():
            other_copy(i).wait_recv()
            far[r] = (near_ref[3, r].astype(f32) + other[r].astype(f32)).astype(jnp.bfloat16)

        @pl.when(me >= 2)
        def _():
            far_copy(i).start()

    loop(send_far)
    q_copy.wait()

    def quarter(k, carry):
        total[k] = lax.dot_general(dq_ref[...], q_mat[k], last, preferred_element_type=f32)
        return carry

    lax.fori_loop(0, total.shape[0], quarter, 0)

    def send_mid(i):
        r = rows(i)
        beside_copy(i).wait_recv()
        mid[r] = (near_ref[1, r].astype(f32) + beside[r].astype(f32)).astype(jnp.bfloat16)

        @pl.when(me + 2 < n)
        def _():
            far_copy(i).wait_recv()
            mid[r] = (
                near_ref[1, r].astype(f32) + beside[r].astype(f32) + far_in[r].astype(f32)
            ).astype(jnp.bfloat16)

        @pl.when(me >= 2)
        def _():
            mid_copy(i).start()

    loop(send_mid)
    kv_copy.wait()

    def pass_on(i):
        r = rows(i)
        mate_pass_copy(i).wait_recv()
        stage[r] = (part[pass_q, r].astype(f32) + from_core[0, r].astype(f32)).astype(jnp.bfloat16)
        y_copy(i).start()

    def middle(i):
        r = rows(i)
        own[r] = down_ref[r]

        @pl.when(odd == 0)
        def _():
            other_copy(i).wait_recv()
            own[r] = own[r] + other[r].astype(f32)

        @pl.when(me + 2 < n)
        def _():
            mid_copy(i).wait_recv()
            own[r] = own[r] + mid_in[r].astype(f32)

        pieces = []
        for g in range(half // width):
            cols = slice(g * width, (g + 1) * width)
            pieces.append(
                rotate_back(
                    lin_ref[r, cols], gain_ref[...], cos_ref[r], sin_ref[r], own[r, cols]
                ).astype(jnp.bfloat16)
            )
        pieces.append(own[r, half:].astype(jnp.bfloat16))
        dkv = jnp.concatenate(pieces, axis=1)

        def product(k):
            part[k, r] = (
                total[k, r]
                + lax.dot_general(dkv, kv_mat[k], last, preferred_element_type=f32)
            ).astype(jnp.bfloat16)

        product(mate_pass_q)
        mate_pass_copy(i).start()
        product(pass_q)
        product(mate_keep_q)
        mate_keep_copy(i).start()

        @pl.when(i > 0)
        def _():
            pass_on(i - 1)

        product(keep_q)

    loop(middle)
    pass_on(CUTS - 1)

    def finish(i):
        r = rows(i)
        mate_keep_copy(i).wait_recv()
        y_copy(i).wait_recv()
        out_ref[r] = (
            part[keep_q, r].astype(f32) + from_core[1, r].astype(f32) + from_y[r].astype(f32)
        ).astype(jnp.bfloat16)
        mate_pass_copy(i).wait_send()
        mate_keep_copy(i).wait_send()
        y_copy(i).wait_send()
        other_copy(i).wait_send()
        beside_copy(i).wait_send()

        @pl.when(me >= 2)
        def _():
            far_copy(i).wait_send()
            mid_copy(i).wait_send()

    loop(finish)


def tail(n, near, down, lin, gain, cosine, sine, dq, q_mat, kv_mat):
    heads, wide, q_cols = q_mat.shape
    tok_rows = lin.shape[0]
    hbm = pl.BlockSpec(memory_space=pl.ANY)
    bf16 = jnp.bfloat16
    block = (tok_rows, wide)
    return pl.pallas_call(
        functools.partial(tail_kernel, n),
        out_shape=jax.ShapeDtypeStruct(block, bf16),
        in_specs=[VMEM] * 7 + [hbm] * 2,
        out_specs=VMEM,
        scratch_shapes=[
            pltpu.VMEM(q_mat.shape, bf16),
            pltpu.VMEM(kv_mat.shape, bf16),
            pltpu.VMEM((heads,) + block, jnp.float32),
            pltpu.VMEM((heads,) + block, bf16),
            pltpu.VMEM(down.shape, jnp.float32),
        ]
        + [pltpu.VMEM(down.shape, bf16)] * 6
        + [
            pltpu.VMEM((2,) + block, bf16),
            pltpu.VMEM(block, bf16),
            pltpu.VMEM(block, bf16),
            pltpu.SemaphoreType.DMA((4, CUTS)),
            pltpu.SemaphoreType.DMA((4, CUTS)),
            pltpu.SemaphoreType.DMA((3, CUTS)),
            pltpu.SemaphoreType.DMA((3, CUTS)),
            pltpu.SemaphoreType.DMA((2,)),
        ],
        compiler_params=pltpu.CompilerParams(
            collective_id=2, has_side_effects=True, vmem_limit_bytes=48 * 1024 * 1024
        ),
    )(near, down, lin, gain, cosine, sine, dq, q_mat, kv_mat)


def attend_kernel(
    reach,
    kv_heads,
    scale,
    there_ref,
    windows_ref,
    lin_ref,
    own_ref,
    near_ref,
    cot_ref,
    gain_ref,
    cos_ref,
    sin_ref,
    attn_ref,
    dq_ref,
    down_ref,
    dnear_ref,
    keys,
    soft,
    acc,
):
    rows = own_ref.shape[0]
    width = gain_ref.shape[1]
    q_heads = lin_ref.shape[1] // width
    group = q_heads // kv_heads
    keys[0] = own_ref[...]
    for step in range(1, reach + 1):
        keys[step] = jnp.where(there_ref[step - 1] > 0, near_ref[step - 1], 0)
    acc[...] = jnp.zeros_like(acc)
    gap = lax.broadcasted_iota(jnp.int32, (rows, rows), 0) - lax.broadcasted_iota(
        jnp.int32, (rows, rows), 1
    )
    last = (((1,), (1,)), ((), ()))
    first = (((0,), (0,)), ((), ()))

    def head(h, carry):
        cols = pl.ds(pl.multiple_of(h * width, width), width)
        kcols = pl.ds(pl.multiple_of(h // group * width, width), width)
        vcols = pl.ds(pl.multiple_of((kv_heads + h // group) * width, width), width)
        u = lin_ref[:, cols]
        q = rotate(u, gain_ref[...], cos_ref[...], sin_ref[...]).astype(jnp.bfloat16)
        cot = cot_ref[:, cols]
        peak = jnp.full((rows, 1), -1e30, jnp.float32)
        for b in range(reach + 1):
            s = scale * lax.dot_general(
                q, keys[b, :, kcols], last, preferred_element_type=jnp.float32
            )
            distance = gap + b * rows
            limit = windows_ref[h]
            if b == 0:
                ok = (distance >= 0) & (distance < limit)
            else:
                ok = distance < jnp.where(there_ref[b - 1] > 0, limit, 0)
            s = jnp.where(ok, s, -1e30)
            soft[b] = s
            peak = jnp.maximum(peak, jnp.max(s, axis=-1, keepdims=True))
        total = jnp.zeros((rows, 1), jnp.float32)
        for b in range(reach + 1):
            e = jnp.exp(soft[b] - peak)
            soft[b] = e
            total = total + jnp.sum(e, axis=-1, keepdims=True)
        inverse = 1.0 / total
        out = jnp.zeros((rows, width), jnp.float32)
        for b in range(reach + 1):
            p = soft[b] * inverse
            soft[b] = p
            pb = p.astype(jnp.bfloat16)
            out = out + jnp.dot(pb, keys[b, :, vcols], preferred_element_type=jnp.float32)
            acc[b, :, vcols] += lax.dot_general(
                pb, cot, first, preferred_element_type=jnp.float32
            )
        out = out.astype(jnp.bfloat16)
        attn_ref[:, cols] = out
        delta = jnp.sum(
            cot.astype(jnp.float32) * out.astype(jnp.float32), axis=-1, keepdims=True
        )
        dq = jnp.zeros((rows, width), jnp.float32)
        for b in range(reach + 1):
            dp = lax.dot_general(
                cot, keys[b, :, vcols], last, preferred_element_type=jnp.float32
            )
            ds = (soft[b] * (dp - delta)).astype(jnp.bfloat16)
            dq = dq + jnp.dot(ds, keys[b, :, kcols], preferred_element_type=jnp.float32)
            acc[b, :, kcols] += scale * lax.dot_general(
                ds, q, first, preferred_element_type=jnp.float32
            )
        dq_ref[:, cols] = rotate_back(
            u, gain_ref[...], cos_ref[...], sin_ref[...], scale * dq
        ).astype(jnp.bfloat16)
        return carry

    lax.fori_loop(0, q_heads, head, 0)
    down_ref[...] = acc[0]
    for step in range(1, reach + 1):
        dnear_ref[step - 1] = acc[step].astype(jnp.bfloat16)


VMEM = pl.BlockSpec(memory_space=pltpu.VMEM)
SMEM = pl.BlockSpec(memory_space=pltpu.SMEM)
ROOM = pltpu.CompilerParams(vmem_limit_bytes=40 * 1024 * 1024)


def body(
    tokens,
    q_weight,
    k_weight,
    v_weight,
    q_gain,
    k_gain,
    windows,
    token_weight,
    loss_mask,
    grad_attn,
):
    n = lax.axis_size("seq")
    me = lax.axis_index("seq")
    tok_rows, depth = tokens.shape
    head_width = q_gain.shape[0]
    q_cols = q_weight.shape[1]
    kv_cols = 2 * k_weight.shape[1]
    kv_heads = k_weight.shape[1] // head_width
    reach = WINDOW // tok_rows
    scale = QPRE ** (-0.5)
    f32 = jnp.float32

    kept = token_weight * loss_mask.astype(f32)
    tile = jnp.broadcast_to(jnp.sum(kept), (8, 128))
    kv_full, tiles = kv_gather(n, k_weight, v_weight, tile)
    positions = me * tok_rows + jnp.arange(tok_rows, dtype=jnp.int32)
    half_width = head_width // 2
    frequency = 10000.0 ** (-(jnp.arange(half_width, dtype=f32) * 2.0) / head_width)
    angles = positions.astype(f32)[:, None] * frequency[None, :]
    cosine, sine = jnp.cos(angles), jnp.sin(angles)
    cosine = jnp.concatenate([cosine, cosine], axis=1)
    sine = jnp.concatenate([-sine, sine], axis=1)
    steps = jnp.arange(1, reach + 1, dtype=jnp.int32)
    before = (me >= steps).astype(jnp.int32)
    q_gain = q_gain[None, :]
    k_gain = k_gain[None, :]

    kv_matrix = kv_full.reshape(depth, kv_cols)
    kv_lin = jnp.dot(tokens, kv_matrix, preferred_element_type=f32)
    kv_own, cot = pl.pallas_call(
        functools.partial(kv_ready_kernel, float(tok_rows * n)),
        out_shape=[
            jax.ShapeDtypeStruct((tok_rows, kv_cols), jnp.bfloat16),
            jax.ShapeDtypeStruct((tok_rows, q_cols), jnp.bfloat16),
        ],
        in_specs=[VMEM] * 7,
        out_specs=[VMEM] * 2,
        compiler_params=ROOM,
    )(kv_lin, k_gain, cosine, sine, tiles, kept[:, None], grad_attn)
    q_full, near = q_gather(n, reach, q_weight, kv_own)
    q_matrix = q_full.reshape(depth, q_cols)
    q_lin = jnp.dot(tokens, q_matrix, preferred_element_type=f32)
    attended, dq_lin, down, dnear = pl.pallas_call(
        functools.partial(attend_kernel, reach, kv_heads, scale),
        out_shape=[
            jax.ShapeDtypeStruct((tok_rows, q_cols), jnp.bfloat16),
            jax.ShapeDtypeStruct((tok_rows, q_cols), jnp.bfloat16),
            jax.ShapeDtypeStruct((tok_rows, kv_cols), f32),
            jax.ShapeDtypeStruct((reach, tok_rows, kv_cols), jnp.bfloat16),
        ],
        in_specs=[SMEM] * 2 + [VMEM] * 7,
        out_specs=[VMEM] * 4,
        scratch_shapes=[
            pltpu.VMEM((reach + 1, tok_rows, kv_cols), jnp.bfloat16),
            pltpu.VMEM((reach + 1, tok_rows, tok_rows), f32),
            pltpu.VMEM((reach + 1, tok_rows, kv_cols), f32),
        ],
        compiler_params=ROOM,
    )(before, windows, q_lin, kv_own, near, cot, q_gain, cosine, sine)
    heads = lax.axis_size("head")
    grad_tokens = tail(
        n,
        dnear,
        down,
        kv_lin,
        k_gain,
        cosine,
        sine,
        dq_lin,
        q_full.reshape(heads, depth // heads, q_cols),
        kv_full.reshape(heads, depth // heads, kv_cols),
    )
    return (attended, grad_tokens)


def solution(mesh):
    in_specs = (
        P("seq", None),
        P("seq", "head"),
        P("seq", "head"),
        P("seq", "head"),
        P(),
        P(),
        P("head"),
        P("seq"),
        P("seq"),
        P("seq", "head"),
    )
    out_specs = (P("seq", "head"), P("seq", "head"))
    return jax.shard_map(body, mesh=mesh, in_specs=in_specs, out_specs=out_specs, check_vma=False)
```

```python
import functools

import jax
import jax.numpy as jnp
from jax import lax
from jax.experimental import pallas as pl
from jax.experimental.pallas import tpu as pltpu
from jax.sharding import PartitionSpec as P

QPRE = 168
WINDOW = 1024
NORM_EPS = 1e-06
MESH = pl.DeviceIdType.MESH


def ring_place(index, n):
    return jnp.where(index % 2 == 0, index // 2, n - 1 - index // 2)


def ring_index(place, n):
    return jnp.where(place < n // 2, 2 * place, 2 * (n - 1 - place) + 1)


def row_cuts(rows, parts):
    if rows % 16 or rows < 16 * parts:
        return [(0, rows)]
    units = rows // 16
    edges = [16 * (units * i // parts) for i in range(parts + 1)]
    return [(a, b - a) for a, b in zip(edges, edges[1:])]


def ring_gather(n, jobs, me, send_sems, recv_sems, middle, hooks=()):
    place = ring_place(me, n)

    def at(distance):
        return ring_index(lax.rem(place + distance + n, n), n)

    def copy(step, job):
        source, dest, way = jobs[job]
        owner = at(-way * step)
        return pltpu.make_async_remote_copy(
            src_ref=dest(owner),
            dst_ref=dest(owner),
            send_sem=send_sems.at[step, job],
            recv_sem=recv_sems.at[step, job],
            device_id={"seq": at(way)},
            device_id_type=MESH,
        )

    def first(job):
        source, dest, way = jobs[job]
        return pltpu.make_async_remote_copy(
            src_ref=source,
            dst_ref=dest(me),
            send_sem=send_sems.at[0, job],
            recv_sem=recv_sems.at[0, job],
            device_id={"seq": at(way)},
            device_id_type=MESH,
        )

    for job in range(len(jobs)):
        first(job).start()
    middle()

    def arrived(step, job):
        source, dest, way = jobs[job]
        owner = at(-way * (step + 1))
        return pltpu.make_async_remote_copy(
            src_ref=dest(owner),
            dst_ref=dest(owner),
            send_sem=send_sems.at[step, job],
            recv_sem=recv_sems.at[step, job],
            device_id={"seq": at(way)},
            device_id_type=MESH,
        )

    def body(step, carry):
        for job in range(len(jobs)):
            arrived(step - 1, job).wait_recv()
            copy(step, job).start()
        return carry

    done = 1
    for turn, hook in hooks:
        lax.fori_loop(done, turn, body, 0)
        hook()
        done = turn
    lax.fori_loop(done, n - 1, body, 0)
    for job in range(len(jobs)):
        arrived(n - 2, job).wait_recv()

    def drain(step, carry):
        for job in range(len(jobs)):
            arrived(step, job).wait_send()
        return carry

    lax.fori_loop(0, n - 1, drain, 0)


def greet(peers):
    barrier = pltpu.get_barrier_semaphore()
    for peer in peers:
        pl.semaphore_signal(barrier, inc=1, device_id={"seq": peer}, device_id_type=MESH)
    pl.semaphore_wait(barrier, len(peers))


def greet_near(n, me, more=0):
    barrier = pltpu.get_barrier_semaphore()

    def signal(peer):
        pl.semaphore_signal(barrier, inc=1, device_id={"seq": peer}, device_id_type=MESH)

    signal(pair_of(me))

    @pl.when(me + 2 < n)
    def _():
        signal(me + 2)

    @pl.when(me >= 2)
    def _():
        signal(me - 2)

    pl.semaphore_wait(barrier, more + 1 + jnp.minimum(me // 2, 1) + jnp.minimum((n - 1 - me) // 2, 1))


def pair_of(me):
    return me + 1 - 2 * (me % 2)


def to_seq(source, dest, peer, send, recv):
    return pltpu.make_async_remote_copy(
        src_ref=source,
        dst_ref=dest,
        send_sem=send,
        recv_sem=recv,
        device_id={"seq": peer},
        device_id_type=MESH,
    )


def kv_gather_kernel(n, k_ref, v_ref, tile_ref, kv_out, tile_out, send, recv, local):
    me = lax.axis_index("seq")
    rows, width = k_ref.shape
    place = ring_place(me, n)
    greet([ring_index(lax.rem(place + d + n, n), n) for d in (1, -1)])
    own = [
        pltpu.make_async_copy(k_ref, kv_out.at[me, :, pl.ds(0, width)], local.at[0]),
        pltpu.make_async_copy(v_ref, kv_out.at[me, :, pl.ds(width, width)], local.at[1]),
        pltpu.make_async_copy(tile_ref, tile_out.at[me], local.at[2]),
    ]
    jobs = []
    for a, size in row_cuts(rows, 2):
        jobs.append(
            (
                k_ref.at[pl.ds(a, size)],
                lambda owner, a=a, size=size: kv_out.at[owner, pl.ds(a, size), pl.ds(0, width)],
                1,
            )
        )
        jobs.append(
            (
                v_ref.at[pl.ds(a, size)],
                lambda owner, a=a, size=size: kv_out.at[owner, pl.ds(a, size), pl.ds(width, width)],
                -1,
            )
        )
    jobs.append((tile_ref, lambda owner: tile_out.at[owner], 1))

    def middle():
        for c in own:
            c.start()

    ring_gather(n, jobs, me, send, recv, middle)
    for c in own:
        c.wait()


def kv_gather(n, k_weight, v_weight, tile):
    rows, width = k_weight.shape
    jobs = 2 * len(row_cuts(rows, 2)) + 1
    hbm = pl.BlockSpec(memory_space=pl.ANY)
    return pl.pallas_call(
        functools.partial(kv_gather_kernel, n),
        out_shape=[
            jax.ShapeDtypeStruct((n, rows, 2 * width), jnp.bfloat16),
            jax.ShapeDtypeStruct((n,) + tile.shape, jnp.float32),
        ],
        in_specs=[hbm] * 3,
        out_specs=[hbm] * 2,
        scratch_shapes=[
            pltpu.SemaphoreType.DMA((n - 1, jobs)),
            pltpu.SemaphoreType.DMA((n - 1, jobs)),
            pltpu.SemaphoreType.DMA((3,)),
        ],
        compiler_params=pltpu.CompilerParams(collective_id=0, has_side_effects=True),
    )(k_weight, v_weight, tile)


def q_gather_kernel(n, q_ref, kv_ref, q_out, near_out, *sems):
    greet_near(n, lax.axis_index("seq"))
    q_and_near(n, q_ref, kv_ref, q_out, near_out, *sems)


def q_and_near(n, q_ref, kv_ref, q_out, near_out, send, recv, nsend, nrecv, local, ready=None):
    me = lax.axis_index("seq")
    odd = me % 2
    rows = q_ref.shape[0]
    own = pltpu.make_async_copy(q_ref, q_out.at[me], local.at[0])
    pair = pair_of(me)
    up = to_seq(kv_ref, near_out.at[1], me + 2, nsend.at[0], nrecv.at[1])
    across = to_seq(kv_ref, near_out.at[0], pair, nsend.at[1], nrecv.at[0])
    up_again = to_seq(near_out.at[1], near_out.at[3], me + 2, nsend.at[2], nrecv.at[3])
    slot = 2 - 2 * odd
    across_two = to_seq(near_out.at[1], near_out.at[slot], pair, nsend.at[3], nrecv.at[slot])
    across_four = to_seq(near_out.at[3], near_out.at[2], pair, nsend.at[4], nrecv.at[2])
    has_up = me + 2 < n
    jobs = []
    for i, (a, size) in enumerate(row_cuts(rows, 4)):
        jobs.append(
            (
                q_ref.at[pl.ds(a, size)],
                lambda owner, a=a, size=size: q_out.at[owner, pl.ds(a, size)],
                1 if i % 2 == 0 else -1,
            )
        )

    def middle():
        own.start()
        if ready is not None:
            ready()
        pl.when(has_up)(up.start)
        pl.when(odd == 0)(across.start)

    def soon():
        @pl.when(me >= 2)
        def _():
            up.wait_recv()
            across_two.start()
            pl.when(has_up)(up_again.start)

    def later():
        @pl.when(me >= 4)
        def _():
            up_again.wait_recv()
            pl.when(odd == 1)(across_four.start)

    ring_gather(n, jobs, me, send, recv, middle, ((2, soon), (4, later)))
    own.wait()

    @pl.when(has_up)
    def _():
        up.wait_send()
        pl.when(me >= 2)(up_again.wait_send)

    pl.when(me >= 2)(across_two.wait_send)

    @pl.when(odd == 0)
    def _():
        across.wait_send()
        pl.when(me >= 2)(lambda: to_seq(kv_ref, near_out.at[0], pair, nsend.at[1], nrecv.at[0]).wait_recv())
        pl.when(me >= 4)(across_four.wait_recv)

    @pl.when(odd == 1)
    def _():
        across.wait_recv()
        pl.when(me >= 4)(across_four.wait_send)
        pl.when(me >= 2)(lambda: to_seq(kv_ref, near_out.at[2], pair, nsend.at[1], nrecv.at[2]).wait_recv())


def q_gather(n, reach, q_weight, kv_own):
    rows, width = q_weight.shape
    jobs = len(row_cuts(rows, 4))
    hbm = pl.BlockSpec(memory_space=pl.ANY)
    return pl.pallas_call(
        functools.partial(q_gather_kernel, n),
        out_shape=[
            jax.ShapeDtypeStruct((n, rows, width), jnp.bfloat16),
            jax.ShapeDtypeStruct((reach,) + kv_own.shape, jnp.bfloat16),
        ],
        in_specs=[hbm] * 2,
        out_specs=[hbm] * 2,
        scratch_shapes=[
            pltpu.SemaphoreType.DMA((n - 1, jobs)),
            pltpu.SemaphoreType.DMA((n - 1, jobs)),
            pltpu.SemaphoreType.DMA((5,)),
            pltpu.SemaphoreType.DMA((reach,)),
            pltpu.SemaphoreType.DMA((1,)),
        ],
        compiler_params=pltpu.CompilerParams(collective_id=1, has_side_effects=True),
    )(q_weight, kv_own)


CUTS = 4


def swap_halves(x):
    half = x.shape[-1] // 2
    return jnp.concatenate([x[:, half:], x[:, :half]], axis=1)


def rotate(u, gain, cosine, sine):
    mean_square = jnp.mean(u * u, axis=-1, keepdims=True)
    m = u * lax.rsqrt(mean_square + NORM_EPS) * gain
    return m * cosine + swap_halves(m) * sine


def rotate_back(u, gain, cosine, sine, grad):
    r = lax.rsqrt(jnp.mean(u * u, axis=-1, keepdims=True) + NORM_EPS)
    dn = (grad * cosine + swap_halves(grad * sine)) * gain
    return r * dn - u * (r * r * r) * jnp.mean(u * dn, axis=-1, keepdims=True)


def kv_ready_kernel(
    tokens_total, lin_ref, gain_ref, cos_ref, sin_ref, tiles_ref, kept_ref, grad_ref, out_ref, cot_ref
):
    width = gain_ref.shape[1]
    half = lin_ref.shape[1] // 2
    for g in range(half // width):
        cols = slice(g * width, (g + 1) * width)
        out_ref[:, cols] = rotate(
            lin_ref[:, cols], gain_ref[...], cos_ref[...], sin_ref[...]
        ).astype(jnp.bfloat16)
    out_ref[:, half:] = lin_ref[:, half:].astype(jnp.bfloat16)
    normalizer = jnp.sum(tiles_ref[...], axis=0)[0:1, 0:1]
    factor = kept_ref[...] * (tokens_total / normalizer)
    cot_ref[...] = (grad_ref[...].astype(jnp.float32) * factor).astype(jnp.bfloat16)


def front_kernel(
    n,
    tokens_total,
    k_ref,
    v_ref,
    tile_ref,
    q_ref,
    tokens_ref,
    gain_ref,
    cos_ref,
    sin_ref,
    kept_ref,
    grad_ref,
    kv_out,
    q_out,
    near_out,
    lin_ref,
    own_ref,
    cot_ref,
    tiles,
    ksend,
    krecv,
    klocal,
    *sems,
):
    me = lax.axis_index("seq")
    rows, width = k_ref.shape
    greet_near(n, me)

    def block(owner, a=0, size=rows):
        return pl.ds(pl.multiple_of(owner * rows + a, 16), size)

    own = [
        pltpu.make_async_copy(k_ref, kv_out.at[block(me), pl.ds(0, width)], klocal.at[0]),
        pltpu.make_async_copy(v_ref, kv_out.at[block(me), pl.ds(width, width)], klocal.at[1]),
        pltpu.make_async_copy(tile_ref, tiles.at[me], klocal.at[2]),
    ]
    jobs = []
    for a, size in row_cuts(rows, 2):
        for ref, col, way in ((k_ref, 0, 1), (v_ref, width, -1)):
            jobs.append(
                (
                    ref.at[pl.ds(a, size)],
                    lambda owner, a=a, size=size, col=col: kv_out.at[
                        block(owner, a, size), pl.ds(col, width)
                    ],
                    way,
                )
            )
    jobs.append((tile_ref, lambda owner: tiles.at[owner], 1))

    def begin():
        for c in own:
            c.start()

    ring_gather(n, jobs, me, ksend, krecv, begin)
    for c in own:
        c.wait()
    step = 384

    def ready():
        lin_ref[...] = jnp.zeros_like(lin_ref)

        def product(i, carry):
            part = pl.ds(pl.multiple_of(i * step, step), step)
            lin_ref[...] += jnp.dot(
                tokens_ref[:, part], kv_out[part, :], preferred_element_type=jnp.float32
            )
            return carry

        lax.fori_loop(0, n * rows // step, product, 0)
        kv_ready_kernel(
            tokens_total, lin_ref, gain_ref, cos_ref, sin_ref, tiles, kept_ref, grad_ref, own_ref, cot_ref
        )

    q_and_near(n, q_ref, own_ref, q_out, near_out, *sems, ready=ready)


def front(n, reach, k_weight, v_weight, tile, q_weight, tokens, gain, cosine, sine, kept, grad):
    rows, width = k_weight.shape
    q_cols = q_weight.shape[1]
    tok_rows = tokens.shape[0]
    kv_jobs = 2 * len(row_cuts(rows, 2)) + 1
    q_jobs = len(row_cuts(rows, 4))
    hbm = pl.BlockSpec(memory_space=pl.ANY)
    bf16 = jnp.bfloat16
    dma = pltpu.SemaphoreType.DMA
    return pl.pallas_call(
        functools.partial(front_kernel, n, float(tok_rows * n)),
        out_shape=[
            jax.ShapeDtypeStruct((n * rows, 2 * width), bf16),
            jax.ShapeDtypeStruct((n, rows, q_cols), bf16),
            jax.ShapeDtypeStruct((reach, tok_rows, 2 * width), bf16),
            jax.ShapeDtypeStruct((tok_rows, 2 * width), jnp.float32),
            jax.ShapeDtypeStruct((tok_rows, 2 * width), bf16),
            jax.ShapeDtypeStruct((tok_rows, q_cols), bf16),
        ],
        in_specs=[hbm] * 2 + [VMEM, hbm] + [VMEM] * 6,
        out_specs=[VMEM, hbm, hbm] + [VMEM] * 3,
        scratch_shapes=[
            pltpu.VMEM((n,) + tile.shape, jnp.float32),
            dma((n - 1, kv_jobs)),
            dma((n - 1, kv_jobs)),
            dma((3,)),
            dma((n - 1, q_jobs)),
            dma((n - 1, q_jobs)),
            dma((5,)),
            dma((reach,)),
            dma((1,)),
        ],
        compiler_params=pltpu.CompilerParams(
            collective_id=0, has_side_effects=True, vmem_limit_bytes=40 * 1024 * 1024
        ),
    )(k_weight, v_weight, tile, q_weight, tokens, gain, cosine, sine, kept, grad)


def tail_kernel(
    n,
    near_ref,
    down_ref,
    lin_ref,
    gain_ref,
    cos_ref,
    sin_ref,
    dq_ref,
    q_hbm,
    kv_hbm,
    out_ref,
    q_mat,
    kv_mat,
    total,
    part,
    own,
    beside,
    other,
    far_in,
    far,
    mid,
    mid_in,
    from_core,
    stage,
    from_y,
    send,
    recv,
    hsend,
    hrecv,
    local,
):
    me = lax.axis_index("seq")
    odd = me % 2
    pair = pair_of(me)
    h = lax.axis_index("head")
    core, y = h % 2, h // 2
    mate = 2 * y + 1 - core
    across = 2 * (1 - y) + core
    size = near_ref.shape[1] // CUTS
    width = gain_ref.shape[1]
    half = lin_ref.shape[1] // 2
    f32 = jnp.float32
    last = (((1,), (1,)), ((), ()))
    q_copy = pltpu.make_async_copy(q_hbm, q_mat, local.at[0])
    kv_copy = pltpu.make_async_copy(kv_hbm, kv_mat, local.at[1])
    q_copy.start()
    kv_copy.start()
    barrier = pltpu.get_barrier_semaphore()
    for peer in (mate, across):
        pl.semaphore_signal(barrier, inc=1, device_id={"head": peer}, device_id_type=MESH)
    greet_near(n, me, 2)

    def rows(i):
        return pl.ds(pl.multiple_of(i * size, size), size)

    def to_head(source, dest, peer, kind, i):
        return pltpu.make_async_remote_copy(
            src_ref=source,
            dst_ref=dest,
            send_sem=hsend.at[kind, i],
            recv_sem=hrecv.at[kind, i],
            device_id={"head": peer},
            device_id_type=MESH,
        )

    def other_copy(i):
        r = rows(i)
        return to_seq(near_ref.at[2 - 2 * odd, r], other.at[r], pair, send.at[0, i], recv.at[0, i])

    def beside_copy(i):
        r = rows(i)
        return to_seq(near_ref.at[2 * odd, r], beside.at[r], pair, send.at[1, i], recv.at[1, i])

    def far_copy(i):
        r = rows(i)
        return to_seq(far.at[r], far_in.at[r], me - 2, send.at[2, i], recv.at[2, i])

    def mid_copy(i):
        r = rows(i)
        return to_seq(mid.at[r], mid_in.at[r], me - 2, send.at[3, i], recv.at[3, i])

    pass_q, keep_q = 2 * (1 - y) + core, 2 * y + core
    mate_pass_q, mate_keep_q = 2 * (1 - y) + 1 - core, 2 * y + 1 - core

    def mate_pass_copy(i):
        r = rows(i)
        return to_head(part.at[mate_pass_q, r], from_core.at[0, r], mate, 0, i)

    def mate_keep_copy(i):
        r = rows(i)
        return to_head(part.at[mate_keep_q, r], from_core.at[1, r], mate, 1, i)

    def y_copy(i):
        r = rows(i)
        return to_head(stage.at[r], from_y.at[r], across, 2, i)

    def loop(step):
        lax.fori_loop(0, CUTS, lambda i, c: (step(i), c)[1], 0)

    def begin(i):
        other_copy(i).start()
        beside_copy(i).start()

    loop(begin)

    def send_far(i):
        r = rows(i)
        far[r] = near_ref[3, r]

        @pl.when(odd == 1)
        def _():
            other_copy(i).wait_recv()
            far[r] = (near_ref[3, r].astype(f32) + other[r].astype(f32)).astype(jnp.bfloat16)

        @pl.when(me >= 2)
        def _():
            far_copy(i).start()

    loop(send_far)
    q_copy.wait()

    def quarter(k, carry):
        total[k] = lax.dot_general(dq_ref[...], q_mat[k], last, preferred_element_type=f32)
        return carry

    lax.fori_loop(0, total.shape[0], quarter, 0)

    def send_mid(i):
        r = rows(i)
        beside_copy(i).wait_recv()
        mid[r] = (near_ref[1, r].astype(f32) + beside[r].astype(f32)).astype(jnp.bfloat16)

        @pl.when(me + 2 < n)
        def _():
            far_copy(i).wait_recv()
            mid[r] = (
                near_ref[1, r].astype(f32) + beside[r].astype(f32) + far_in[r].astype(f32)
            ).astype(jnp.bfloat16)

        @pl.when(me >= 2)
        def _():
            mid_copy(i).start()

    loop(send_mid)
    kv_copy.wait()

    def pass_on(i):
        r = rows(i)
        mate_pass_copy(i).wait_recv()
        stage[r] = (part[pass_q, r].astype(f32) + from_core[0, r].astype(f32)).astype(jnp.bfloat16)
        y_copy(i).start()

    def middle(i):
        r = rows(i)
        own[r] = down_ref[r]

        @pl.when(odd == 0)
        def _():
            other_copy(i).wait_recv()
            own[r] = own[r] + other[r].astype(f32)

        @pl.when(me + 2 < n)
        def _():
            mid_copy(i).wait_recv()
            own[r] = own[r] + mid_in[r].astype(f32)

        pieces = []
        for g in range(half // width):
            cols = slice(g * width, (g + 1) * width)
            pieces.append(
                rotate_back(
                    lin_ref[r, cols], gain_ref[...], cos_ref[r], sin_ref[r], own[r, cols]
                ).astype(jnp.bfloat16)
            )
        pieces.append(own[r, half:].astype(jnp.bfloat16))
        dkv = jnp.concatenate(pieces, axis=1)

        def product(k):
            part[k, r] = (
                total[k, r]
                + lax.dot_general(dkv, kv_mat[k], last, preferred_element_type=f32)
            ).astype(jnp.bfloat16)

        product(mate_pass_q)
        mate_pass_copy(i).start()
        product(pass_q)
        product(mate_keep_q)
        mate_keep_copy(i).start()

        @pl.when(i > 0)
        def _():
            pass_on(i - 1)

        product(keep_q)

    loop(middle)
    pass_on(CUTS - 1)

    def finish(i):
        r = rows(i)
        mate_keep_copy(i).wait_recv()
        y_copy(i).wait_recv()
        out_ref[r] = (
            part[keep_q, r].astype(f32) + from_core[1, r].astype(f32) + from_y[r].astype(f32)
        ).astype(jnp.bfloat16)
        mate_pass_copy(i).wait_send()
        mate_keep_copy(i).wait_send()
        y_copy(i).wait_send()
        other_copy(i).wait_send()
        beside_copy(i).wait_send()

        @pl.when(me >= 2)
        def _():
            far_copy(i).wait_send()
            mid_copy(i).wait_send()

    loop(finish)


def tail(n, near, down, lin, gain, cosine, sine, dq, q_mat, kv_mat):
    heads, wide, q_cols = q_mat.shape
    tok_rows = lin.shape[0]
    hbm = pl.BlockSpec(memory_space=pl.ANY)
    bf16 = jnp.bfloat16
    block = (tok_rows, wide)
    return pl.pallas_call(
        functools.partial(tail_kernel, n),
        out_shape=jax.ShapeDtypeStruct(block, bf16),
        in_specs=[VMEM] * 7 + [hbm] * 2,
        out_specs=VMEM,
        scratch_shapes=[
            pltpu.VMEM(q_mat.shape, bf16),
            pltpu.VMEM(kv_mat.shape, bf16),
            pltpu.VMEM((heads,) + block, jnp.float32),
            pltpu.VMEM((heads,) + block, bf16),
            pltpu.VMEM(down.shape, jnp.float32),
        ]
        + [pltpu.VMEM(down.shape, bf16)] * 6
        + [
            pltpu.VMEM((2,) + block, bf16),
            pltpu.VMEM(block, bf16),
            pltpu.VMEM(block, bf16),
            pltpu.SemaphoreType.DMA((4, CUTS)),
            pltpu.SemaphoreType.DMA((4, CUTS)),
            pltpu.SemaphoreType.DMA((3, CUTS)),
            pltpu.SemaphoreType.DMA((3, CUTS)),
            pltpu.SemaphoreType.DMA((2,)),
        ],
        compiler_params=pltpu.CompilerParams(
            collective_id=2, has_side_effects=True, vmem_limit_bytes=48 * 1024 * 1024
        ),
    )(near, down, lin, gain, cosine, sine, dq, q_mat, kv_mat)


def attend_kernel(
    reach,
    kv_heads,
    scale,
    there_ref,
    windows_ref,
    lin_ref,
    own_ref,
    near_ref,
    cot_ref,
    gain_ref,
    cos_ref,
    sin_ref,
    attn_ref,
    dq_ref,
    down_ref,
    dnear_ref,
    keys,
    soft,
    acc,
):
    rows = own_ref.shape[0]
    width = gain_ref.shape[1]
    q_heads = lin_ref.shape[1] // width
    group = q_heads // kv_heads
    keys[0] = own_ref[...]
    for step in range(1, reach + 1):
        keys[step] = jnp.where(there_ref[step - 1] > 0, near_ref[step - 1], 0)
    acc[...] = jnp.zeros_like(acc)
    gap = lax.broadcasted_iota(jnp.int32, (rows, rows), 0) - lax.broadcasted_iota(
        jnp.int32, (rows, rows), 1
    )
    last = (((1,), (1,)), ((), ()))
    first = (((0,), (0,)), ((), ()))

    def head(h, carry):
        cols = pl.ds(pl.multiple_of(h * width, width), width)
        kcols = pl.ds(pl.multiple_of(h // group * width, width), width)
        vcols = pl.ds(pl.multiple_of((kv_heads + h // group) * width, width), width)
        u = lin_ref[:, cols]
        q = rotate(u, gain_ref[...], cos_ref[...], sin_ref[...]).astype(jnp.bfloat16)
        cot = cot_ref[:, cols]
        peak = jnp.full((rows, 1), -1e30, jnp.float32)
        for b in range(reach + 1):
            s = scale * lax.dot_general(
                q, keys[b, :, kcols], last, preferred_element_type=jnp.float32
            )
            distance = gap + b * rows
            limit = windows_ref[h]
            if b == 0:
                ok = (distance >= 0) & (distance < limit)
            else:
                ok = distance < jnp.where(there_ref[b - 1] > 0, limit, 0)
            s = jnp.where(ok, s, -1e30)
            soft[b] = s
            peak = jnp.maximum(peak, jnp.max(s, axis=-1, keepdims=True))
        total = jnp.zeros((rows, 1), jnp.float32)
        for b in range(reach + 1):
            e = jnp.exp(soft[b] - peak)
            soft[b] = e
            total = total + jnp.sum(e, axis=-1, keepdims=True)
        inverse = 1.0 / total
        out = jnp.zeros((rows, width), jnp.float32)
        for b in range(reach + 1):
            p = soft[b] * inverse
            soft[b] = p
            pb = p.astype(jnp.bfloat16)
            out = out + jnp.dot(pb, keys[b, :, vcols], preferred_element_type=jnp.float32)
            acc[b, :, vcols] += lax.dot_general(
                pb, cot, first, preferred_element_type=jnp.float32
            )
        out = out.astype(jnp.bfloat16)
        attn_ref[:, cols] = out
        delta = jnp.sum(
            cot.astype(jnp.float32) * out.astype(jnp.float32), axis=-1, keepdims=True
        )
        dq = jnp.zeros((rows, width), jnp.float32)
        for b in range(reach + 1):
            dp = lax.dot_general(
                cot, keys[b, :, vcols], last, preferred_element_type=jnp.float32
            )
            ds = (soft[b] * (dp - delta)).astype(jnp.bfloat16)
            dq = dq + jnp.dot(ds, keys[b, :, kcols], preferred_element_type=jnp.float32)
            acc[b, :, kcols] += scale * lax.dot_general(
                ds, q, first, preferred_element_type=jnp.float32
            )
        dq_ref[:, cols] = rotate_back(
            u, gain_ref[...], cos_ref[...], sin_ref[...], scale * dq
        ).astype(jnp.bfloat16)
        return carry

    lax.fori_loop(0, q_heads, head, 0)
    down_ref[...] = acc[0]
    for step in range(1, reach + 1):
        dnear_ref[step - 1] = acc[step].astype(jnp.bfloat16)


VMEM = pl.BlockSpec(memory_space=pltpu.VMEM)
SMEM = pl.BlockSpec(memory_space=pltpu.SMEM)
ROOM = pltpu.CompilerParams(vmem_limit_bytes=40 * 1024 * 1024)


def body(
    tokens,
    q_weight,
    k_weight,
    v_weight,
    q_gain,
    k_gain,
    windows,
    token_weight,
    loss_mask,
    grad_attn,
):
    n = lax.axis_size("seq")
    me = lax.axis_index("seq")
    tok_rows, depth = tokens.shape
    head_width = q_gain.shape[0]
    q_cols = q_weight.shape[1]
    kv_cols = 2 * k_weight.shape[1]
    kv_heads = k_weight.shape[1] // head_width
    reach = WINDOW // tok_rows
    scale = QPRE ** (-0.5)
    f32 = jnp.float32

    kept = token_weight * loss_mask.astype(f32)
    tile = jnp.broadcast_to(jnp.sum(kept), (8, 128))
    positions = me * tok_rows + jnp.arange(tok_rows, dtype=jnp.int32)
    half_width = head_width // 2
    frequency = 10000.0 ** (-(jnp.arange(half_width, dtype=f32) * 2.0) / head_width)
    angles = positions.astype(f32)[:, None] * frequency[None, :]
    cosine, sine = jnp.cos(angles), jnp.sin(angles)
    cosine = jnp.concatenate([cosine, cosine], axis=1)
    sine = jnp.concatenate([-sine, sine], axis=1)
    steps = jnp.arange(1, reach + 1, dtype=jnp.int32)
    before = (me >= steps).astype(jnp.int32)
    q_gain = q_gain[None, :]
    k_gain = k_gain[None, :]

    if k_weight.shape[0] % 16 == 0 and depth % 384 == 0:
        kv_full, q_full, near, kv_lin, kv_own, cot = front(
            n,
            reach,
            k_weight,
            v_weight,
            tile,
            q_weight,
            tokens,
            k_gain,
            cosine,
            sine,
            kept[:, None],
            grad_attn,
        )
    else:
        kv_full, tiles = kv_gather(n, k_weight, v_weight, tile)
        kv_matrix = kv_full.reshape(depth, kv_cols)
        kv_lin = jnp.dot(tokens, kv_matrix, preferred_element_type=f32)
        kv_own, cot = pl.pallas_call(
            functools.partial(kv_ready_kernel, float(tok_rows * n)),
            out_shape=[
                jax.ShapeDtypeStruct((tok_rows, kv_cols), jnp.bfloat16),
                jax.ShapeDtypeStruct((tok_rows, q_cols), jnp.bfloat16),
            ],
            in_specs=[VMEM] * 7,
            out_specs=[VMEM] * 2,
            compiler_params=ROOM,
        )(kv_lin, k_gain, cosine, sine, tiles, kept[:, None], grad_attn)
        q_full, near = q_gather(n, reach, q_weight, kv_own)
    q_matrix = q_full.reshape(depth, q_cols)
    q_lin = jnp.dot(tokens, q_matrix, preferred_element_type=f32)
    attended, dq_lin, down, dnear = pl.pallas_call(
        functools.partial(attend_kernel, reach, kv_heads, scale),
        out_shape=[
            jax.ShapeDtypeStruct((tok_rows, q_cols), jnp.bfloat16),
            jax.ShapeDtypeStruct((tok_rows, q_cols), jnp.bfloat16),
            jax.ShapeDtypeStruct((tok_rows, kv_cols), f32),
            jax.ShapeDtypeStruct((reach, tok_rows, kv_cols), jnp.bfloat16),
        ],
        in_specs=[SMEM] * 2 + [VMEM] * 7,
        out_specs=[VMEM] * 4,
        scratch_shapes=[
            pltpu.VMEM((reach + 1, tok_rows, kv_cols), jnp.bfloat16),
            pltpu.VMEM((reach + 1, tok_rows, tok_rows), f32),
            pltpu.VMEM((reach + 1, tok_rows, kv_cols), f32),
        ],
        compiler_params=ROOM,
    )(before, windows, q_lin, kv_own, near, cot, q_gain, cosine, sine)
    heads = lax.axis_size("head")
    grad_tokens = tail(
        n,
        dnear,
        down,
        kv_lin,
        k_gain,
        cosine,
        sine,
        dq_lin,
        q_full.reshape(heads, depth // heads, q_cols),
        kv_full.reshape(heads, depth // heads, kv_cols),
    )
    return (attended, grad_tokens)


def solution(mesh):
    in_specs = (
        P("seq", None),
        P("seq", "head"),
        P("seq", "head"),
        P("seq", "head"),
        P(),
        P(),
        P("head"),
        P("seq"),
        P("seq"),
        P("seq", "head"),
    )
    out_specs = (P("seq", "head"), P("seq", "head"))
    return jax.shard_map(body, mesh=mesh, in_specs=in_specs, out_specs=out_specs, check_vma=False)
```

```python
import functools

import jax
import jax.numpy as jnp
from jax import lax
from jax.experimental import pallas as pl
from jax.experimental.pallas import tpu as pltpu
from jax.sharding import PartitionSpec as P

QPRE = 168
WINDOW = 1024
NORM_EPS = 1e-06
MESH = pl.DeviceIdType.MESH


def ring_place(index, n):
    return jnp.where(index % 2 == 0, index // 2, n - 1 - index // 2)


def ring_index(place, n):
    return jnp.where(place < n // 2, 2 * place, 2 * (n - 1 - place) + 1)


def row_cuts(rows, parts):
    if rows % 16 or rows < 16 * parts:
        return [(0, rows)]
    units = rows // 16
    edges = [16 * (units * i // parts) for i in range(parts + 1)]
    return [(a, b - a) for a, b in zip(edges, edges[1:])]


def ring_gather(n, jobs, me, send_sems, recv_sems, middle, hooks=()):
    place = ring_place(me, n)

    def at(distance):
        return ring_index(lax.rem(place + distance + n, n), n)

    def copy(step, job):
        source, dest, way = jobs[job]
        owner = at(-way * step)
        return pltpu.make_async_remote_copy(
            src_ref=dest(owner),
            dst_ref=dest(owner),
            send_sem=send_sems.at[step, job],
            recv_sem=recv_sems.at[step, job],
            device_id={"seq": at(way)},
            device_id_type=MESH,
        )

    def first(job):
        source, dest, way = jobs[job]
        return pltpu.make_async_remote_copy(
            src_ref=source,
            dst_ref=dest(me),
            send_sem=send_sems.at[0, job],
            recv_sem=recv_sems.at[0, job],
            device_id={"seq": at(way)},
            device_id_type=MESH,
        )

    for job in range(len(jobs)):
        first(job).start()
    middle()

    def arrived(step, job):
        source, dest, way = jobs[job]
        owner = at(-way * (step + 1))
        return pltpu.make_async_remote_copy(
            src_ref=dest(owner),
            dst_ref=dest(owner),
            send_sem=send_sems.at[step, job],
            recv_sem=recv_sems.at[step, job],
            device_id={"seq": at(way)},
            device_id_type=MESH,
        )

    def body(step, carry):
        for job in range(len(jobs)):
            arrived(step - 1, job).wait_recv()
            copy(step, job).start()
        return carry

    done = 1
    for turn, hook in hooks:
        lax.fori_loop(done, turn, body, 0)
        hook()
        done = turn
    lax.fori_loop(done, n - 1, body, 0)
    for job in range(len(jobs)):
        arrived(n - 2, job).wait_recv()

    def drain(step, carry):
        for job in range(len(jobs)):
            arrived(step, job).wait_send()
        return carry

    lax.fori_loop(0, n - 1, drain, 0)


def greet(peers):
    barrier = pltpu.get_barrier_semaphore()
    for peer in peers:
        pl.semaphore_signal(barrier, inc=1, device_id={"seq": peer}, device_id_type=MESH)
    pl.semaphore_wait(barrier, len(peers))


def greet_near(n, me, more=0):
    barrier = pltpu.get_barrier_semaphore()

    def signal(peer):
        pl.semaphore_signal(barrier, inc=1, device_id={"seq": peer}, device_id_type=MESH)

    signal(pair_of(me))

    @pl.when(me + 2 < n)
    def _():
        signal(me + 2)

    @pl.when(me >= 2)
    def _():
        signal(me - 2)

    pl.semaphore_wait(barrier, more + 1 + jnp.minimum(me // 2, 1) + jnp.minimum((n - 1 - me) // 2, 1))


def pair_of(me):
    return me + 1 - 2 * (me % 2)


def to_seq(source, dest, peer, send, recv):
    return pltpu.make_async_remote_copy(
        src_ref=source,
        dst_ref=dest,
        send_sem=send,
        recv_sem=recv,
        device_id={"seq": peer},
        device_id_type=MESH,
    )


def kv_gather_kernel(n, k_ref, v_ref, tile_ref, kv_out, tile_out, send, recv, local):
    me = lax.axis_index("seq")
    rows, width = k_ref.shape
    place = ring_place(me, n)
    greet([ring_index(lax.rem(place + d + n, n), n) for d in (1, -1)])
    own = [
        pltpu.make_async_copy(k_ref, kv_out.at[me, :, pl.ds(0, width)], local.at[0]),
        pltpu.make_async_copy(v_ref, kv_out.at[me, :, pl.ds(width, width)], local.at[1]),
        pltpu.make_async_copy(tile_ref, tile_out.at[me], local.at[2]),
    ]
    jobs = []
    for a, size in row_cuts(rows, 2):
        jobs.append(
            (
                k_ref.at[pl.ds(a, size)],
                lambda owner, a=a, size=size: kv_out.at[owner, pl.ds(a, size), pl.ds(0, width)],
                1,
            )
        )
        jobs.append(
            (
                v_ref.at[pl.ds(a, size)],
                lambda owner, a=a, size=size: kv_out.at[owner, pl.ds(a, size), pl.ds(width, width)],
                -1,
            )
        )
    jobs.append((tile_ref, lambda owner: tile_out.at[owner], 1))

    def middle():
        for c in own:
            c.start()

    ring_gather(n, jobs, me, send, recv, middle)
    for c in own:
        c.wait()


def kv_gather(n, k_weight, v_weight, tile):
    rows, width = k_weight.shape
    jobs = 2 * len(row_cuts(rows, 2)) + 1
    hbm = pl.BlockSpec(memory_space=pl.ANY)
    return pl.pallas_call(
        functools.partial(kv_gather_kernel, n),
        out_shape=[
            jax.ShapeDtypeStruct((n, rows, 2 * width), jnp.bfloat16),
            jax.ShapeDtypeStruct((n,) + tile.shape, jnp.float32),
        ],
        in_specs=[hbm] * 3,
        out_specs=[hbm] * 2,
        scratch_shapes=[
            pltpu.SemaphoreType.DMA((n - 1, jobs)),
            pltpu.SemaphoreType.DMA((n - 1, jobs)),
            pltpu.SemaphoreType.DMA((3,)),
        ],
        compiler_params=pltpu.CompilerParams(collective_id=0, has_side_effects=True),
    )(k_weight, v_weight, tile)


def q_gather_kernel(n, q_ref, kv_ref, q_out, near_out, *sems):
    greet_near(n, lax.axis_index("seq"))
    q_and_near(n, q_ref, kv_ref, q_out, near_out, *sems)


def q_and_near(n, q_ref, kv_ref, q_out, near_out, send, recv, nsend, nrecv, local, ready=None):
    me = lax.axis_index("seq")
    odd = me % 2
    rows = q_ref.shape[0]
    own = pltpu.make_async_copy(q_ref, q_out.at[me], local.at[0])
    pair = pair_of(me)
    up = to_seq(kv_ref, near_out.at[1], me + 2, nsend.at[0], nrecv.at[1])
    across = to_seq(kv_ref, near_out.at[0], pair, nsend.at[1], nrecv.at[0])
    up_again = to_seq(near_out.at[1], near_out.at[3], me + 2, nsend.at[2], nrecv.at[3])
    slot = 2 - 2 * odd
    across_two = to_seq(near_out.at[1], near_out.at[slot], pair, nsend.at[3], nrecv.at[slot])
    across_four = to_seq(near_out.at[3], near_out.at[2], pair, nsend.at[4], nrecv.at[2])
    has_up = me + 2 < n
    jobs = []
    for i, (a, size) in enumerate(row_cuts(rows, 4)):
        jobs.append(
            (
                q_ref.at[pl.ds(a, size)],
                lambda owner, a=a, size=size: q_out.at[owner, pl.ds(a, size)],
                1 if i % 2 == 0 else -1,
            )
        )

    def middle():
        own.start()
        if ready is not None:
            ready()
        pl.when(has_up)(up.start)
        pl.when(odd == 0)(across.start)

    def soon():
        @pl.when(me >= 2)
        def _():
            up.wait_recv()
            across_two.start()
            pl.when(has_up)(up_again.start)

    def later():
        @pl.when(me >= 4)
        def _():
            up_again.wait_recv()
            pl.when(odd == 1)(across_four.start)

    ring_gather(n, jobs, me, send, recv, middle, ((2, soon), (4, later)))
    own.wait()

    @pl.when(has_up)
    def _():
        up.wait_send()
        pl.when(me >= 2)(up_again.wait_send)

    pl.when(me >= 2)(across_two.wait_send)

    @pl.when(odd == 0)
    def _():
        across.wait_send()
        pl.when(me >= 2)(lambda: to_seq(kv_ref, near_out.at[0], pair, nsend.at[1], nrecv.at[0]).wait_recv())
        pl.when(me >= 4)(across_four.wait_recv)

    @pl.when(odd == 1)
    def _():
        across.wait_recv()
        pl.when(me >= 4)(across_four.wait_send)
        pl.when(me >= 2)(lambda: to_seq(kv_ref, near_out.at[2], pair, nsend.at[1], nrecv.at[2]).wait_recv())


def q_gather(n, reach, q_weight, kv_own):
    rows, width = q_weight.shape
    jobs = len(row_cuts(rows, 4))
    hbm = pl.BlockSpec(memory_space=pl.ANY)
    return pl.pallas_call(
        functools.partial(q_gather_kernel, n),
        out_shape=[
            jax.ShapeDtypeStruct((n, rows, width), jnp.bfloat16),
            jax.ShapeDtypeStruct((reach,) + kv_own.shape, jnp.bfloat16),
        ],
        in_specs=[hbm] * 2,
        out_specs=[hbm] * 2,
        scratch_shapes=[
            pltpu.SemaphoreType.DMA((n - 1, jobs)),
            pltpu.SemaphoreType.DMA((n - 1, jobs)),
            pltpu.SemaphoreType.DMA((5,)),
            pltpu.SemaphoreType.DMA((reach,)),
            pltpu.SemaphoreType.DMA((1,)),
        ],
        compiler_params=pltpu.CompilerParams(collective_id=1, has_side_effects=True),
    )(q_weight, kv_own)


CUTS = 4


def swap_halves(x):
    half = x.shape[-1] // 2
    return jnp.concatenate([x[:, half:], x[:, :half]], axis=1)


def rotate(u, gain, cosine, sine):
    mean_square = jnp.mean(u * u, axis=-1, keepdims=True)
    m = u * lax.rsqrt(mean_square + NORM_EPS) * gain
    return m * cosine + swap_halves(m) * sine


def rotate_back(u, gain, cosine, sine, grad):
    r = lax.rsqrt(jnp.mean(u * u, axis=-1, keepdims=True) + NORM_EPS)
    dn = (grad * cosine + swap_halves(grad * sine)) * gain
    return r * dn - u * (r * r * r) * jnp.mean(u * dn, axis=-1, keepdims=True)


def kv_ready_kernel(
    tokens_total, lin_ref, gain_ref, cos_ref, sin_ref, tiles_ref, kept_ref, grad_ref, out_ref, cot_ref
):
    width = gain_ref.shape[1]
    half = lin_ref.shape[1] // 2
    for g in range(half // width):
        cols = slice(g * width, (g + 1) * width)
        out_ref[:, cols] = rotate(
            lin_ref[:, cols], gain_ref[...], cos_ref[...], sin_ref[...]
        ).astype(jnp.bfloat16)
    out_ref[:, half:] = lin_ref[:, half:].astype(jnp.bfloat16)
    normalizer = jnp.sum(tiles_ref[...], axis=0)[0:1, 0:1]
    factor = kept_ref[...] * (tokens_total / normalizer)
    cot_ref[...] = (grad_ref[...].astype(jnp.float32) * factor).astype(jnp.bfloat16)


def front_kernel(
    n,
    tokens_total,
    k_ref,
    v_ref,
    tile_ref,
    q_ref,
    tokens_hbm,
    gain_ref,
    cos_hbm,
    sin_hbm,
    kept_ref,
    grad_hbm,
    kv_out,
    q_out,
    near_out,
    lin_ref,
    own_ref,
    cot_ref,
    tiles,
    tokens_ref,
    cos_ref,
    sin_ref,
    grad_ref,
    ksend,
    krecv,
    klocal,
    *sems,
):
    me = lax.axis_index("seq")
    rows, width = k_ref.shape
    greet_near(n, me)

    def block(owner, a=0, size=rows):
        return pl.ds(pl.multiple_of(owner * rows + a, 16), size)

    own = [
        pltpu.make_async_copy(k_ref, kv_out.at[block(me), pl.ds(0, width)], klocal.at[0]),
        pltpu.make_async_copy(v_ref, kv_out.at[block(me), pl.ds(width, width)], klocal.at[1]),
        pltpu.make_async_copy(tile_ref, tiles.at[me], klocal.at[2]),
        pltpu.make_async_copy(tokens_hbm, tokens_ref, klocal.at[3]),
        pltpu.make_async_copy(cos_hbm, cos_ref, klocal.at[4]),
        pltpu.make_async_copy(sin_hbm, sin_ref, klocal.at[5]),
        pltpu.make_async_copy(grad_hbm, grad_ref, klocal.at[6]),
    ]
    jobs = []
    for a, size in row_cuts(rows, 2):
        for ref, col, way in ((k_ref, 0, 1), (v_ref, width, -1)):
            jobs.append(
                (
                    ref.at[pl.ds(a, size)],
                    lambda owner, a=a, size=size, col=col: kv_out.at[
                        block(owner, a, size), pl.ds(col, width)
                    ],
                    way,
                )
            )
    jobs.append((tile_ref, lambda owner: tiles.at[owner], 1))

    def begin():
        for c in own:
            c.start()

    ring_gather(n, jobs, me, ksend, krecv, begin)
    for c in own:
        c.wait()
    step = 384

    def ready():
        lin_ref[...] = jnp.zeros_like(lin_ref)

        def product(i, carry):
            part = pl.ds(pl.multiple_of(i * step, step), step)
            lin_ref[...] += jnp.dot(
                tokens_ref[:, part], kv_out[part, :], preferred_element_type=jnp.float32
            )
            return carry

        lax.fori_loop(0, n * rows // step, product, 0)
        kv_ready_kernel(
            tokens_total, lin_ref, gain_ref, cos_ref, sin_ref, tiles, kept_ref, grad_ref, own_ref, cot_ref
        )

    q_and_near(n, q_ref, own_ref, q_out, near_out, *sems, ready=ready)


def front(n, reach, k_weight, v_weight, tile, q_weight, tokens, gain, cosine, sine, kept, grad):
    rows, width = k_weight.shape
    q_cols = q_weight.shape[1]
    tok_rows = tokens.shape[0]
    kv_jobs = 2 * len(row_cuts(rows, 2)) + 1
    q_jobs = len(row_cuts(rows, 4))
    hbm = pl.BlockSpec(memory_space=pl.ANY)
    bf16 = jnp.bfloat16
    dma = pltpu.SemaphoreType.DMA
    return pl.pallas_call(
        functools.partial(front_kernel, n, float(tok_rows * n)),
        out_shape=[
            jax.ShapeDtypeStruct((n * rows, 2 * width), bf16),
            jax.ShapeDtypeStruct((n, rows, q_cols), bf16),
            jax.ShapeDtypeStruct((reach, tok_rows, 2 * width), bf16),
            jax.ShapeDtypeStruct((tok_rows, 2 * width), jnp.float32),
            jax.ShapeDtypeStruct((tok_rows, 2 * width), bf16),
            jax.ShapeDtypeStruct((tok_rows, q_cols), bf16),
        ],
        in_specs=[hbm] * 2 + [VMEM, hbm, hbm, VMEM, hbm, hbm, VMEM, hbm],
        out_specs=[VMEM, hbm, hbm] + [VMEM] * 3,
        scratch_shapes=[
            pltpu.VMEM((n,) + tile.shape, jnp.float32),
            pltpu.VMEM(tokens.shape, bf16),
            pltpu.VMEM(cosine.shape, jnp.float32),
            pltpu.VMEM(sine.shape, jnp.float32),
            pltpu.VMEM(grad.shape, bf16),
            dma((n - 1, kv_jobs)),
            dma((n - 1, kv_jobs)),
            dma((7,)),
            dma((n - 1, q_jobs)),
            dma((n - 1, q_jobs)),
            dma((5,)),
            dma((reach,)),
            dma((1,)),
        ],
        compiler_params=pltpu.CompilerParams(
            collective_id=0, has_side_effects=True, vmem_limit_bytes=40 * 1024 * 1024
        ),
    )(k_weight, v_weight, tile, q_weight, tokens, gain, cosine, sine, kept, grad)


def tail_kernel(
    n,
    near_ref,
    down_ref,
    lin_ref,
    gain_ref,
    cos_ref,
    sin_ref,
    dq_ref,
    q_hbm,
    kv_hbm,
    out_ref,
    q_mat,
    kv_mat,
    total,
    part,
    own,
    beside,
    other,
    far_in,
    far,
    mid,
    mid_in,
    from_core,
    stage,
    from_y,
    send,
    recv,
    hsend,
    hrecv,
    local,
):
    me = lax.axis_index("seq")
    odd = me % 2
    pair = pair_of(me)
    h = lax.axis_index("head")
    core, y = h % 2, h // 2
    mate = 2 * y + 1 - core
    across = 2 * (1 - y) + core
    size = near_ref.shape[1] // CUTS
    width = gain_ref.shape[1]
    half = lin_ref.shape[1] // 2
    f32 = jnp.float32
    last = (((1,), (1,)), ((), ()))
    q_copy = pltpu.make_async_copy(q_hbm, q_mat, local.at[0])
    kv_copy = pltpu.make_async_copy(kv_hbm, kv_mat, local.at[1])
    q_copy.start()
    kv_copy.start()
    barrier = pltpu.get_barrier_semaphore()
    for peer in (mate, across):
        pl.semaphore_signal(barrier, inc=1, device_id={"head": peer}, device_id_type=MESH)
    greet_near(n, me, 2)

    def rows(i):
        return pl.ds(pl.multiple_of(i * size, size), size)

    def to_head(source, dest, peer, kind, i):
        return pltpu.make_async_remote_copy(
            src_ref=source,
            dst_ref=dest,
            send_sem=hsend.at[kind, i],
            recv_sem=hrecv.at[kind, i],
            device_id={"head": peer},
            device_id_type=MESH,
        )

    def other_copy(i):
        r = rows(i)
        return to_seq(near_ref.at[2 - 2 * odd, r], other.at[r], pair, send.at[0, i], recv.at[0, i])

    def beside_copy(i):
        r = rows(i)
        return to_seq(near_ref.at[2 * odd, r], beside.at[r], pair, send.at[1, i], recv.at[1, i])

    def far_copy(i):
        r = rows(i)
        return to_seq(far.at[r], far_in.at[r], me - 2, send.at[2, i], recv.at[2, i])

    def mid_copy(i):
        r = rows(i)
        return to_seq(mid.at[r], mid_in.at[r], me - 2, send.at[3, i], recv.at[3, i])

    pass_q, keep_q = 2 * (1 - y) + core, 2 * y + core
    mate_pass_q, mate_keep_q = 2 * (1 - y) + 1 - core, 2 * y + 1 - core

    def mate_pass_copy(i):
        r = rows(i)
        return to_head(part.at[mate_pass_q, r], from_core.at[0, r], mate, 0, i)

    def mate_keep_copy(i):
        r = rows(i)
        return to_head(part.at[mate_keep_q, r], from_core.at[1, r], mate, 1, i)

    def y_copy(i):
        r = rows(i)
        return to_head(stage.at[r], from_y.at[r], across, 2, i)

    def loop(step):
        lax.fori_loop(0, CUTS, lambda i, c: (step(i), c)[1], 0)

    def begin(i):
        other_copy(i).start()
        beside_copy(i).start()

    loop(begin)

    def send_far(i):
        r = rows(i)
        far[r] = near_ref[3, r]

        @pl.when(odd == 1)
        def _():
            other_copy(i).wait_recv()
            far[r] = (near_ref[3, r].astype(f32) + other[r].astype(f32)).astype(jnp.bfloat16)

        @pl.when(me >= 2)
        def _():
            far_copy(i).start()

    loop(send_far)
    q_copy.wait()

    def quarter(k, carry):
        total[k] = lax.dot_general(dq_ref[...], q_mat[k], last, preferred_element_type=f32)
        return carry

    lax.fori_loop(0, total.shape[0], quarter, 0)

    def send_mid(i):
        r = rows(i)
        beside_copy(i).wait_recv()
        mid[r] = (near_ref[1, r].astype(f32) + beside[r].astype(f32)).astype(jnp.bfloat16)

        @pl.when(me + 2 < n)
        def _():
            far_copy(i).wait_recv()
            mid[r] = (
                near_ref[1, r].astype(f32) + beside[r].astype(f32) + far_in[r].astype(f32)
            ).astype(jnp.bfloat16)

        @pl.when(me >= 2)
        def _():
            mid_copy(i).start()

    loop(send_mid)
    kv_copy.wait()

    def pass_on(i):
        r = rows(i)
        mate_pass_copy(i).wait_recv()
        stage[r] = (part[pass_q, r].astype(f32) + from_core[0, r].astype(f32)).astype(jnp.bfloat16)
        y_copy(i).start()

    def middle(i):
        r = rows(i)
        own[r] = down_ref[r]

        @pl.when(odd == 0)
        def _():
            other_copy(i).wait_recv()
            own[r] = own[r] + other[r].astype(f32)

        @pl.when(me + 2 < n)
        def _():
            mid_copy(i).wait_recv()
            own[r] = own[r] + mid_in[r].astype(f32)

        pieces = []
        for g in range(half // width):
            cols = slice(g * width, (g + 1) * width)
            pieces.append(
                rotate_back(
                    lin_ref[r, cols], gain_ref[...], cos_ref[r], sin_ref[r], own[r, cols]
                ).astype(jnp.bfloat16)
            )
        pieces.append(own[r, half:].astype(jnp.bfloat16))
        dkv = jnp.concatenate(pieces, axis=1)

        def product(k):
            part[k, r] = (
                total[k, r]
                + lax.dot_general(dkv, kv_mat[k], last, preferred_element_type=f32)
            ).astype(jnp.bfloat16)

        product(mate_pass_q)
        mate_pass_copy(i).start()
        product(pass_q)
        product(mate_keep_q)
        mate_keep_copy(i).start()

        @pl.when(i > 0)
        def _():
            pass_on(i - 1)

        product(keep_q)

    loop(middle)
    pass_on(CUTS - 1)

    def finish(i):
        r = rows(i)
        mate_keep_copy(i).wait_recv()
        y_copy(i).wait_recv()
        out_ref[r] = (
            part[keep_q, r].astype(f32) + from_core[1, r].astype(f32) + from_y[r].astype(f32)
        ).astype(jnp.bfloat16)
        mate_pass_copy(i).wait_send()
        mate_keep_copy(i).wait_send()
        y_copy(i).wait_send()
        other_copy(i).wait_send()
        beside_copy(i).wait_send()

        @pl.when(me >= 2)
        def _():
            far_copy(i).wait_send()
            mid_copy(i).wait_send()

    loop(finish)


def tail(n, near, down, lin, gain, cosine, sine, dq, q_mat, kv_mat):
    heads, wide, q_cols = q_mat.shape
    tok_rows = lin.shape[0]
    hbm = pl.BlockSpec(memory_space=pl.ANY)
    bf16 = jnp.bfloat16
    block = (tok_rows, wide)
    return pl.pallas_call(
        functools.partial(tail_kernel, n),
        out_shape=jax.ShapeDtypeStruct(block, bf16),
        in_specs=[VMEM] * 7 + [hbm] * 2,
        out_specs=VMEM,
        scratch_shapes=[
            pltpu.VMEM(q_mat.shape, bf16),
            pltpu.VMEM(kv_mat.shape, bf16),
            pltpu.VMEM((heads,) + block, jnp.float32),
            pltpu.VMEM((heads,) + block, bf16),
            pltpu.VMEM(down.shape, jnp.float32),
        ]
        + [pltpu.VMEM(down.shape, bf16)] * 6
        + [
            pltpu.VMEM((2,) + block, bf16),
            pltpu.VMEM(block, bf16),
            pltpu.VMEM(block, bf16),
            pltpu.SemaphoreType.DMA((4, CUTS)),
            pltpu.SemaphoreType.DMA((4, CUTS)),
            pltpu.SemaphoreType.DMA((3, CUTS)),
            pltpu.SemaphoreType.DMA((3, CUTS)),
            pltpu.SemaphoreType.DMA((2,)),
        ],
        compiler_params=pltpu.CompilerParams(
            collective_id=2, has_side_effects=True, vmem_limit_bytes=48 * 1024 * 1024
        ),
    )(near, down, lin, gain, cosine, sine, dq, q_mat, kv_mat)


def attend_kernel(
    reach,
    kv_heads,
    scale,
    there_ref,
    windows_ref,
    lin_ref,
    own_ref,
    near_ref,
    cot_ref,
    gain_ref,
    cos_ref,
    sin_ref,
    attn_ref,
    dq_ref,
    down_ref,
    dnear_ref,
    keys,
    soft,
    acc,
):
    rows = own_ref.shape[0]
    width = gain_ref.shape[1]
    q_heads = lin_ref.shape[1] // width
    group = q_heads // kv_heads
    keys[0] = own_ref[...]
    for step in range(1, reach + 1):
        keys[step] = jnp.where(there_ref[step - 1] > 0, near_ref[step - 1], 0)
    acc[...] = jnp.zeros_like(acc)
    gap = lax.broadcasted_iota(jnp.int32, (rows, rows), 0) - lax.broadcasted_iota(
        jnp.int32, (rows, rows), 1
    )
    last = (((1,), (1,)), ((), ()))
    first = (((0,), (0,)), ((), ()))

    def head(h, carry):
        cols = pl.ds(pl.multiple_of(h * width, width), width)
        kcols = pl.ds(pl.multiple_of(h // group * width, width), width)
        vcols = pl.ds(pl.multiple_of((kv_heads + h // group) * width, width), width)
        u = lin_ref[:, cols]
        q = rotate(u, gain_ref[...], cos_ref[...], sin_ref[...]).astype(jnp.bfloat16)
        cot = cot_ref[:, cols]
        peak = jnp.full((rows, 1), -1e30, jnp.float32)
        for b in range(reach + 1):
            s = scale * lax.dot_general(
                q, keys[b, :, kcols], last, preferred_element_type=jnp.float32
            )
            distance = gap + b * rows
            limit = windows_ref[h]
            if b == 0:
                ok = (distance >= 0) & (distance < limit)
            else:
                ok = distance < jnp.where(there_ref[b - 1] > 0, limit, 0)
            s = jnp.where(ok, s, -1e30)
            soft[b] = s
            peak = jnp.maximum(peak, jnp.max(s, axis=-1, keepdims=True))
        total = jnp.zeros((rows, 1), jnp.float32)
        for b in range(reach + 1):
            e = jnp.exp(soft[b] - peak)
            soft[b] = e
            total = total + jnp.sum(e, axis=-1, keepdims=True)
        inverse = 1.0 / total
        out = jnp.zeros((rows, width), jnp.float32)
        for b in range(reach + 1):
            p = soft[b] * inverse
            soft[b] = p
            pb = p.astype(jnp.bfloat16)
            out = out + jnp.dot(pb, keys[b, :, vcols], preferred_element_type=jnp.float32)
            acc[b, :, vcols] += lax.dot_general(
                pb, cot, first, preferred_element_type=jnp.float32
            )
        out = out.astype(jnp.bfloat16)
        attn_ref[:, cols] = out
        delta = jnp.sum(
            cot.astype(jnp.float32) * out.astype(jnp.float32), axis=-1, keepdims=True
        )
        dq = jnp.zeros((rows, width), jnp.float32)
        for b in range(reach + 1):
            dp = lax.dot_general(
                cot, keys[b, :, vcols], last, preferred_element_type=jnp.float32
            )
            ds = (soft[b] * (dp - delta)).astype(jnp.bfloat16)
            dq = dq + jnp.dot(ds, keys[b, :, kcols], preferred_element_type=jnp.float32)
            acc[b, :, kcols] += scale * lax.dot_general(
                ds, q, first, preferred_element_type=jnp.float32
            )
        dq_ref[:, cols] = rotate_back(
            u, gain_ref[...], cos_ref[...], sin_ref[...], scale * dq
        ).astype(jnp.bfloat16)
        return carry

    lax.fori_loop(0, q_heads, head, 0)
    down_ref[...] = acc[0]
    for step in range(1, reach + 1):
        dnear_ref[step - 1] = acc[step].astype(jnp.bfloat16)


VMEM = pl.BlockSpec(memory_space=pltpu.VMEM)
SMEM = pl.BlockSpec(memory_space=pltpu.SMEM)
ROOM = pltpu.CompilerParams(vmem_limit_bytes=40 * 1024 * 1024)


def body(
    tokens,
    q_weight,
    k_weight,
    v_weight,
    q_gain,
    k_gain,
    windows,
    token_weight,
    loss_mask,
    grad_attn,
):
    n = lax.axis_size("seq")
    me = lax.axis_index("seq")
    tok_rows, depth = tokens.shape
    head_width = q_gain.shape[0]
    q_cols = q_weight.shape[1]
    kv_cols = 2 * k_weight.shape[1]
    kv_heads = k_weight.shape[1] // head_width
    reach = WINDOW // tok_rows
    scale = QPRE ** (-0.5)
    f32 = jnp.float32

    kept = token_weight * loss_mask.astype(f32)
    tile = jnp.broadcast_to(jnp.sum(kept), (8, 128))
    positions = me * tok_rows + jnp.arange(tok_rows, dtype=jnp.int32)
    half_width = head_width // 2
    frequency = 10000.0 ** (-(jnp.arange(half_width, dtype=f32) * 2.0) / head_width)
    angles = positions.astype(f32)[:, None] * frequency[None, :]
    cosine, sine = jnp.cos(angles), jnp.sin(angles)
    cosine = jnp.concatenate([cosine, cosine], axis=1)
    sine = jnp.concatenate([-sine, sine], axis=1)
    steps = jnp.arange(1, reach + 1, dtype=jnp.int32)
    before = (me >= steps).astype(jnp.int32)
    q_gain = q_gain[None, :]
    k_gain = k_gain[None, :]

    if k_weight.shape[0] % 16 == 0 and depth % 384 == 0:
        kv_full, q_full, near, kv_lin, kv_own, cot = front(
            n,
            reach,
            k_weight,
            v_weight,
            tile,
            q_weight,
            tokens,
            k_gain,
            cosine,
            sine,
            kept[:, None],
            grad_attn,
        )
    else:
        kv_full, tiles = kv_gather(n, k_weight, v_weight, tile)
        kv_matrix = kv_full.reshape(depth, kv_cols)
        kv_lin = jnp.dot(tokens, kv_matrix, preferred_element_type=f32)
        kv_own, cot = pl.pallas_call(
            functools.partial(kv_ready_kernel, float(tok_rows * n)),
            out_shape=[
                jax.ShapeDtypeStruct((tok_rows, kv_cols), jnp.bfloat16),
                jax.ShapeDtypeStruct((tok_rows, q_cols), jnp.bfloat16),
            ],
            in_specs=[VMEM] * 7,
            out_specs=[VMEM] * 2,
            compiler_params=ROOM,
        )(kv_lin, k_gain, cosine, sine, tiles, kept[:, None], grad_attn)
        q_full, near = q_gather(n, reach, q_weight, kv_own)
    q_matrix = q_full.reshape(depth, q_cols)
    q_lin = jnp.dot(tokens, q_matrix, preferred_element_type=f32)
    attended, dq_lin, down, dnear = pl.pallas_call(
        functools.partial(attend_kernel, reach, kv_heads, scale),
        out_shape=[
            jax.ShapeDtypeStruct((tok_rows, q_cols), jnp.bfloat16),
            jax.ShapeDtypeStruct((tok_rows, q_cols), jnp.bfloat16),
            jax.ShapeDtypeStruct((tok_rows, kv_cols), f32),
            jax.ShapeDtypeStruct((reach, tok_rows, kv_cols), jnp.bfloat16),
        ],
        in_specs=[SMEM] * 2 + [VMEM] * 7,
        out_specs=[VMEM] * 4,
        scratch_shapes=[
            pltpu.VMEM((reach + 1, tok_rows, kv_cols), jnp.bfloat16),
            pltpu.VMEM((reach + 1, tok_rows, tok_rows), f32),
            pltpu.VMEM((reach + 1, tok_rows, kv_cols), f32),
        ],
        compiler_params=ROOM,
    )(before, windows, q_lin, kv_own, near, cot, q_gain, cosine, sine)
    heads = lax.axis_size("head")
    grad_tokens = tail(
        n,
        dnear,
        down,
        kv_lin,
        k_gain,
        cosine,
        sine,
        dq_lin,
        q_full.reshape(heads, depth // heads, q_cols),
        kv_full.reshape(heads, depth // heads, kv_cols),
    )
    return (attended, grad_tokens)


def solution(mesh):
    in_specs = (
        P("seq", None),
        P("seq", "head"),
        P("seq", "head"),
        P("seq", "head"),
        P(),
        P(),
        P("head"),
        P("seq"),
        P("seq"),
        P("seq", "head"),
    )
    out_specs = (P("seq", "head"), P("seq", "head"))
    return jax.shard_map(body, mesh=mesh, in_specs=in_specs, out_specs=out_specs, check_vma=False)
```
